512 devices in a mesh: mat: 4 (over z_hi), row: 64 (over y, x, core), col: 2 (over z_lo).
Axes of the slice: x: 4, y: 8, z: 8 (z_hi: 4, z_lo: 2; z = z_hi * 2 + z_lo), core: 2. Of those that a mesh axis runs over, the one named last changes fastest.
Arguments:
- iterate: float32 [10752, 10752], P(('mat', 'row'), 'col'), parts along dimension 0, may hold values from -1 to 1, as said below
Outputs:
- update: float32 [10752, 10752], P(('mat', 'row'), 'col'), parts along dimension 0
The draws below stay inside these ranges and needn't reach their ends.
There are 4 independent parts, one for each index of `mat`. The reference program is written for one: setup_inputs(seed, part) draws one part's arguments, and reference() takes and returns one part's arrays. A program takes and returns all parts, laid end to end along the dimension named above; each array names one. Nothing has to cross between parts.
Inputs may be any that keep to these rules, and one draw needn't show every extreme that they name: An iterate of earlier Newton-Schulz steps: a full-rank matrix whose largest singular value is below 2.
All inputs are finite; a program needn't handle non-finite values.
Results may differ from the reference program's by a relative error of at most 0.015.
Values may be sent and summed in bfloat16 or wider, within the bound.
A program may use at most 64 MiB of HBM per device.

```python
import math
import jax
import jax.numpy as jnp
from jax import lax

ROWS = 2688
COLS = 10752


def draw_iterate(key, part):
    key = jax.random.fold_in(key, 11)
    first_key, second_key = jax.random.split(key, 2)
    base_scale = 1.0 / (math.sqrt(ROWS) + math.sqrt(COLS))
    entries = jax.random.normal(first_key, (ROWS, COLS), jnp.float32)
    scales = jnp.exp(jax.random.uniform(second_key, (ROWS, 1), jnp.float32, -0.3, 0.3))
    return (entries * scales * base_scale).astype(jnp.float32)


def setup_inputs(seed: int = 0, part: int = 0) -> dict:
    keys = jax.random.split(jax.random.key(seed), 2)
    part_splits = jax.random.split(jax.random.fold_in(keys[1], part), 2)
    return {
        "iterate": draw_iterate(jax.random.fold_in(jax.random.fold_in(keys[1], part), 71), part),
    }


linear_term = 3.4445
cubic_term = -4.775
quintic_term = 2.0315

def exact_product(former, latter):
    return jnp.dot(former.astype(jnp.float32), latter.astype(jnp.float32), precision=lax.Precision.HIGHEST)

def reference(iterate):
    rounded = iterate.astype(jnp.bfloat16)
    gram = exact_product(rounded, rounded.T).astype(jnp.bfloat16)
    square = exact_product(gram, gram)
    polynomial = (cubic_term * gram.astype(jnp.float32) + quintic_term * square).astype(jnp.bfloat16)
    applied = exact_product(polynomial, rounded)
    return math.sqrt(COLS) * (linear_term * rounded.astype(jnp.float32) + applied)
```

```python
import functools
import math

import jax
import jax.numpy as jnp
from jax import lax
from jax.experimental import pallas as pl
from jax.experimental.pallas import tpu as pltpu
from jax.sharding import PartitionSpec as P

COLS = 10752

linear_term = 3.4445
cubic_term = -4.775
quintic_term = 2.0315

NY = 8
NX = 4
NP = 8
OWN = 42
PAD = 48
DENSE = NY * OWN
TALL = NY * PAD
FULL = NP * DENSE
WIDE = 768
SPLIT = 384
PARTS = ((0, SPLIT), (SPLIT, WIDE - SPLIT))
HALVES = ((0, 1408), (1408, 1280))


def dot(a, b, dims=((1,), (0,))):
    return lax.dot_general(a, b, (dims, ((), ())), preferred_element_type=jnp.float32)


def kernel(x_ref, y_ref, xs, sel, a2a, xg, wg, gp, rb, zs, zr, gf, yp,
           in_s, in_r, ag_s, ag_r, rs_s, rs_r, z_s, z_r, gg_s, gg_r, out_s, out_r):
    m, r, z = lax.axis_index("mat"), lax.axis_index("row"), lax.axis_index("col")
    y, p = r // NP, r % NP
    x, c = p // 2, p % 2
    pending = []

    def dev(yy, xx, cc):
        return (m, (yy % NY) * NP + (xx % NX) * 2 + cc, z)

    def copy(src, dst, ssem, rsem, to):
        return pltpu.make_async_remote_copy(
            src_ref=src, dst_ref=dst, send_sem=ssem, recv_sem=rsem,
            device_id=to, device_id_type=pl.DeviceIdType.MESH)

    def send(src, dst, ssem, rsem, to):
        op = copy(src, dst, ssem, rsem, to)
        op.start()
        pending.append(op)

    def arrive(dst, ssem, rsem, to):
        copy(dst, dst, ssem, rsem, to).wait_recv()

    sibling = dev(y, x, 1 - c)
    east, west = dev(y, x + 1, c), dev(y, x + 3, c)
    other_z = (m, r, 1 - z)
    ydev = [dev(y + k, x, c) for k in range(NY)]

    a2a[:, 640:768] = jnp.zeros((TALL, 128), jnp.bfloat16)
    barrier = pltpu.get_barrier_semaphore()
    for to in ydev[1:] + [sibling, east, west, other_z]:
        pl.semaphore_signal(barrier, inc=1, device_id=to, device_id_type=pl.DeviceIdType.MESH)

    xs[32:48, :] = jnp.zeros((16, xs.shape[1]), jnp.bfloat16)
    xs[0:OWN, :] = x_ref[...].astype(jnp.bfloat16)
    row = lax.broadcasted_iota(jnp.int32, (DENSE, TALL), 0)
    col = lax.broadcasted_iota(jnp.int32, (DENSE, TALL), 1)
    place = row
    for k in range(1, NY):
        place = place + jnp.where(row >= OWN * k, PAD - OWN, 0)
    sel[...] = jnp.where(col == place, 1.0, 0.0).astype(jnp.bfloat16)
    pl.semaphore_wait(barrier, NY + 3)

    def first(yy):
        return pl.multiple_of((21 * yy) // 4 * 128, 128)

    def block(yy):
        return pl.ds(pl.multiple_of((yy % NY) * PAD, 16), PAD)

    def rows(xx, cc):
        return pl.ds(pl.multiple_of(((xx % NX) * 2 + cc) * DENSE, 16), DENSE)

    cuts = ((0, 384), (384, 256), (640, 128))
    order = (4, 3, 5, 2, 6, 1, 7)

    for i, (off, size) in enumerate(cuts):
        for k in order:
            t = (y + k) % NY

            def go(k=k, t=t, i=i, off=off, size=size, start=True):
                op = copy(xs.at[:, pl.ds(pl.multiple_of(first(t) + off, 128), size)],
                          a2a.at[block(y), off:off + size],
                          in_s.at[i, k - 1], in_r.at[i, k - 1], ydev[k])
                if start:
                    op.start()
                else:
                    op.wait_send()
            if i < 2:
                go()
            else:
                pl.when(t % 4 == 3)(go)

    for i, (off, size) in enumerate(cuts):
        def own(off=off, size=size):
            a2a[block(y), off:off + size] = xs[:, pl.ds(pl.multiple_of(first(y) + off, 128), size)]
        if i < 2:
            own()
        else:
            pl.when(y % 4 == 3)(own)

    def in_wait(i):
        off, size = cuts[i]
        for k in order:
            arrive(a2a.at[block(y - k + NY), off:off + size],
                   in_s.at[i, k - 1], in_r.at[i, k - 1], ydev[k])

    def lanes(ch):
        return slice(PARTS[ch][0], PARTS[ch][0] + PARTS[ch][1])

    def gather_start(buf, ch, n):
        mine = buf.at[rows(x, c), lanes(ch)]
        for q, to in enumerate((east, west, sibling)):
            send(mine, mine, ag_s.at[n, ch, q], ag_r.at[n, ch, q], to)

    def gather_end(buf, ch, n):
        def part(xx, cc):
            return buf.at[rows(xx, cc), lanes(ch)]

        def wait(ref, q):
            arrive(ref, ag_s.at[n, ch, q], ag_r.at[n, ch, q], sibling)

        def forward(ref, q, to):
            send(ref, ref, ag_s.at[n, ch, q], ag_r.at[n, ch, q], to)
        wait(part(x + 3, c), 0)
        if ch == 0:
            forward(part(x + 3, c), 3, east)
        forward(part(x + 3, c), 4, sibling)
        wait(part(x + 1, c), 1)
        if ch == 1:
            forward(part(x + 1, c), 3, west)
        forward(part(x + 1, c), 5, sibling)
        wait(part(x + 2, c), 3)
        forward(part(x + 2, c), 6, sibling)
        wait(part(x, 1 - c), 2)
        wait(part(x + 3, 1 - c), 4)
        wait(part(x + 1, 1 - c), 5)
        wait(part(x + 2, 1 - c), 6)

    for ch in range(2):
        in_wait(ch)
        if ch == 1:
            pl.when(y % 4 == 3)(functools.partial(in_wait, 2))
        xg[rows(x, c), lanes(ch)] = dot(sel[...], a2a[:, lanes(ch)]).astype(jnp.bfloat16)
        gather_start(xg, ch, 0)
    for ch in range(2):
        gather_end(xg, ch, 0)

    @pl.loop(0, 7)
    def _(j):
        at = pl.ds(pl.multiple_of(j * 384, 128), 384)
        gp[:, at] = dot(a2a[...], xg[at, :], ((1,), (1,))).astype(jnp.bfloat16)

    def half(h):
        return slice(HALVES[h][0], HALVES[h][0] + HALVES[h][1])

    def f32(v):
        return v.astype(jnp.float32)

    ways = (ydev[1], ydev[NY - 1])
    signs = (1, NY - 1)
    for k in range(4):
        for d in range(2):
            for h in range(2):
                k0 = 0 if d == h else 1
                if k < k0:
                    continue
                t = block(y + signs[d] * (4 - k))
                if k > k0:
                    arrive(rb.at[d, k - 1, :, half(h)], rs_s.at[d, k - 1, h], rs_r.at[d, k - 1, h], ways[d])
                    gp[t, half(h)] = (f32(gp[t, half(h)]) + f32(rb[d, k - 1, :, half(h)])).astype(jnp.bfloat16)
                send(gp.at[t, half(h)], rb.at[d, k, :, half(h)], rs_s.at[d, k, h], rs_r.at[d, k, h], ways[d])
    for h in range(2):
        for d in range(2):
            arrive(rb.at[d, 3, :, half(h)], rs_s.at[d, 3, h], rs_r.at[d, 3, h], ways[d])
        total = f32(gp[block(y), half(h)]) + f32(rb[0, 3, :, half(h)]) + f32(rb[1, 3, :, half(h)])
        zs[:, half(h)] = total.astype(jnp.bfloat16)
        send(zs.at[:, half(h)], zr.at[:, half(h)], z_s.at[h], z_r.at[h], other_z)
    for k in range(4):
        for h in range(2):
            if k == 0:
                arrive(zr.at[:, half(h)], z_s.at[h], z_r.at[h], other_z)
                gf[block(y), half(h)] = (f32(zs[:, half(h)]) + f32(zr[:, half(h)])).astype(jnp.bfloat16)
            for d in range(2):
                ref = gf.at[block(y + (NY - signs[d]) * k), half(h)]
                if k > 0:
                    arrive(ref, gg_s.at[d, k - 1, h], gg_r.at[d, k - 1, h], ways[d])
                if k < 3 or d == h:
                    send(ref, ref, gg_s.at[d, k, h], gg_r.at[d, k, h], ways[d])
    for d in range(2):
        arrive(gf.at[block(y + 4), half(d)], gg_s.at[d, 3, d], gg_r.at[d, 3, d], ways[d])

    for ch in range(2):
        inner = dot(gf[...], xg[:, lanes(ch)])
        inner = cubic_term * f32(a2a[:, lanes(ch)]) + quintic_term * inner
        wg[rows(x, c), lanes(ch)] = dot(sel[...], inner.astype(jnp.bfloat16)).astype(jnp.bfloat16)
        gather_start(wg, ch, 1)

    def out_copy(i, k, src, start_col, to):
        off, size = cuts[i]
        return copy(src.at[:, off:off + size],
                    y_ref.at[:, pl.ds(pl.multiple_of(start_col + off, 128), size)],
                    out_s.at[i, k - 1], out_r.at[i, k - 1], to)

    for ch in range(2):
        gather_end(wg, ch, 1)
        yp[:, lanes(ch)] = dot(gf[...], wg[:, lanes(ch)]).astype(jnp.bfloat16)
        for i in ((0,), (1, 2))[ch]:
            off, size = cuts[i]

            def go(i=i, off=off, size=size):
                for k in order:
                    out_copy(i, k, yp.at[block(y + k), :], first(y), ydev[k]).start()
                y_ref[:, pl.ds(pl.multiple_of(first(y) + off, 128), size)] = yp[block(y), off:off + size]
            if i < 2:
                go()
            else:
                pl.when(y % 4 == 3)(go)

    for i in range(3):
        for k in order:
            src = (y - k + NY) % NY

            def got(i=i, k=k, src=src):
                out_copy(i, k, yp.at[block(y), :], first(src), ydev[k]).wait_recv()
            if i < 2:
                got()
            else:
                pl.when(src % 4 == 3)(got)

    for op in pending:
        op.wait_send()
    for i in range(3):
        for k in order:
            t = (y + k) % NY

            def sent(i=i, k=k, t=t):
                off, size = cuts[i]
                copy(xs.at[:, pl.ds(pl.multiple_of(first(t) + off, 128), size)],
                     a2a.at[block(y), off:off + size],
                     in_s.at[i, k - 1], in_r.at[i, k - 1], ydev[k]).wait_send()

            def left(i=i, k=k):
                out_copy(i, k, yp.at[block(y + k), :], first(y), ydev[k]).wait_send()
            if i < 2:
                sent()
                left()
            else:
                pl.when(t % 4 == 3)(sent)
                pl.when(y % 4 == 3)(left)


def on_device(iterate):
    bf = jnp.bfloat16
    dma = pltpu.SemaphoreType.DMA
    applied = pl.pallas_call(
        kernel,
        out_shape=jax.ShapeDtypeStruct((PAD, iterate.shape[1]), bf),
        in_specs=[pl.BlockSpec(memory_space=pltpu.VMEM)],
        out_specs=pl.BlockSpec(memory_space=pltpu.VMEM),
        scratch_shapes=[
            pltpu.VMEM((PAD, iterate.shape[1]), bf),
            pltpu.VMEM((DENSE, TALL), bf),
            pltpu.VMEM((TALL, WIDE), bf),
            pltpu.VMEM((FULL, WIDE), bf),
            pltpu.VMEM((FULL, WIDE), bf),
            pltpu.VMEM((TALL, FULL), bf),
            pltpu.VMEM((2, 4, PAD, FULL), bf),
            pltpu.VMEM((PAD, FULL), bf),
            pltpu.VMEM((PAD, FULL), bf),
            pltpu.VMEM((TALL, FULL), bf),
            pltpu.VMEM((TALL, WIDE), bf),
            dma((3, 7)), dma((3, 7)),
            dma((2, 2, 7)), dma((2, 2, 7)),
            dma((2, 4, 2)), dma((2, 4, 2)),
            dma((2,)), dma((2,)),
            dma((2, 4, 2)), dma((2, 4, 2)),
            dma((3, 7)), dma((3, 7)),
        ],
        compiler_params=pltpu.CompilerParams(
            collective_id=0, has_side_effects=True, vmem_limit_bytes=50 * 2**20),
        name="newton_schulz",
    )(iterate)
    rounded = iterate.astype(bf).astype(jnp.float32)
    return math.sqrt(COLS) * (linear_term * rounded + applied[:OWN].astype(jnp.float32))


def solution(mesh):
    spec = P(("mat", "row"), "col")
    return jax.shard_map(on_device, mesh=mesh, in_specs=(spec,), out_specs=spec, check_vma=False)
```

```python
import math

import jax
import jax.numpy as jnp
from jax import lax
from jax.experimental import pallas as pl
from jax.experimental.pallas import tpu as pltpu
from jax.sharding import PartitionSpec as P

COLS = 10752

linear_term = 3.4445
cubic_term = -4.775
quintic_term = 2.0315

NY = 8
NX = 4
NP = 8
OWN = 42
PAD = 48
DENSE = NY * OWN
TALL = NY * PAD
FULL = NP * DENSE
WIDE = 768
CHUNK = 256
CUTS = ((0, 256), (256, 256), (512, 128), (640, 128))
ORDER = (4, 3, 5, 2, 6, 1, 7)
STRIPS = ((0, 384, 0), (384, 256, 1), (640, 640, 1), (1280, 640, 0), (1920, 384, 0), (2304, 384, 1))


def dot(a, b, dims=((1,), (0,))):
    return lax.dot_general(a, b, (dims, ((), ())), preferred_element_type=jnp.float32)


def f32(v):
    return v.astype(jnp.float32)


def bf16(v):
    return v.astype(jnp.bfloat16)


def kernel(x_ref, y_ref, xf, xs, sel, a2a, xg, wg, gp, rb, zs, zr, gf, yp, x_sem,
           in_s, in_r, ag_s, ag_r, rs_s, rs_r, z_s, z_r, gg_s, gg_r, out_s, out_r):
    m, r, z = lax.axis_index("mat"), lax.axis_index("row"), lax.axis_index("col")
    y, p = r // NP, r % NP
    x, c = p // 2, p % 2
    pending = []

    def dev(yy, xx, cc):
        return (m, (yy % NY) * NP + (xx % NX) * 2 + cc, z)

    def copy(src, dst, ssem, rsem, to):
        return pltpu.make_async_remote_copy(
            src_ref=src, dst_ref=dst, send_sem=ssem, recv_sem=rsem,
            device_id=to, device_id_type=pl.DeviceIdType.MESH)

    def send(src, dst, ssem, rsem, to):
        op = copy(src, dst, ssem, rsem, to)
        op.start()
        pending.append(op.wait_send)

    def arrive(dst, ssem, rsem, to):
        copy(dst, dst, ssem, rsem, to).wait_recv()

    def when_whole(i, yy, run):
        if i < 3:
            run()
        else:
            pl.when(yy % 4 == 3)(run)

    def launch(op, i, yy):
        when_whole(i, yy, op.start)
        pending.append(lambda: when_whole(i, yy, op.wait_send))

    def drain():
        for wait in pending:
            wait()
        pending.clear()

    sibling = dev(y, x, 1 - c)
    east, west = dev(y, x + 1, c), dev(y, x + 3, c)
    other_z = (m, r, 1 - z)
    ydev = [dev(y + k, x, c) for k in range(NY)]
    ways = (ydev[1], ydev[NY - 1])
    signs = (1, NY - 1)

    fetch = pltpu.make_async_copy(x_ref, xf, x_sem)
    fetch.start()
    a2a[:, 640:768] = jnp.zeros((TALL, 128), jnp.bfloat16)
    barrier = pltpu.get_barrier_semaphore()
    for to in ydev[1:] + [sibling, east, west, other_z]:
        pl.semaphore_signal(barrier, inc=1, device_id=to, device_id_type=pl.DeviceIdType.MESH)

    row = lax.broadcasted_iota(jnp.int32, (DENSE, TALL), 0)
    col = lax.broadcasted_iota(jnp.int32, (DENSE, TALL), 1)
    place = row
    for k in range(1, NY):
        place = place + jnp.where(row >= OWN * k, PAD - OWN, 0)
    sel[...] = bf16(jnp.where(col == place, 1.0, 0.0))
    fetch.wait()
    xs[32:48, :] = jnp.zeros((16, xs.shape[1]), jnp.bfloat16)
    xs[0:OWN, :] = bf16(xf[...])
    pl.semaphore_wait(barrier, NY + 3)

    def first(yy):
        return pl.multiple_of((21 * yy) // 4 * 128, 128)

    def cut(ref, yy, i):
        off, size = CUTS[i]
        return ref.at[:, pl.ds(pl.multiple_of(first(yy) + off, 128), size)]

    def block(yy):
        return pl.ds(pl.multiple_of((yy % NY) * PAD, 16), PAD)

    def in_copy(i, k, src, dst):
        off, size = CUTS[i]
        return copy(cut(xs, src, i), a2a.at[block(dst), off:off + size],
                    in_s.at[i, k - 1], in_r.at[i, k - 1], ydev[k])

    for i in range(4):
        for k in ORDER:
            launch(in_copy(i, k, (y + k) % NY, y), i, (y + k) % NY)

    for i, (off, size) in enumerate(CUTS):
        def own(i=i, off=off, size=size):
            a2a[block(y), off:off + size] = cut(xs, y, i)[...]
        when_whole(i, y, own)

    def in_wait(i):
        for k in ORDER:
            when_whole(i, y, in_copy(i, k, y, y - k + NY).wait_recv)

    def lanes(ch):
        return slice(ch * CHUNK, (ch + 1) * CHUNK)

    class Gather:
        def __init__(self, buf, n, ch):
            self.buf, self.n, self.ch = buf, n, ch

        def ref(self, place, cc, part=None):
            rows = pl.ds(pl.multiple_of((place * 2 + cc) * DENSE, 16), DENSE)
            lo = self.ch * CHUNK
            if part is None:
                return self.buf.at[rows, lo:lo + CHUNK]
            return self.buf.at[rows, lo + part * 128:lo + part * 128 + 128]

        def push(self, q, src, dst, to):
            send(src, dst, ag_s.at[self.n, self.ch, q], ag_r.at[self.n, self.ch, q], to)

        def wait(self, q, ref):
            arrive(ref, ag_s.at[self.n, self.ch, q], ag_r.at[self.n, self.ch, q], sibling)

        def start(self):
            mine = self.ref(0, c)
            self.push(0, mine, self.ref(1, c), east)
            self.push(1, mine, self.ref(2, c), west)
            self.push(2, mine, mine, sibling)

        def near(self):
            self.wait(0, self.ref(1, c))
            self.push(3, self.ref(1, c, 0), self.ref(3, c, 0), east)
            self.push(5, self.ref(1, c), self.ref(1, c), sibling)
            self.wait(1, self.ref(2, c))
            self.push(4, self.ref(2, c, 1), self.ref(3, c, 1), west)
            self.push(6, self.ref(2, c), self.ref(2, c), sibling)

        def far(self):
            self.wait(3, self.ref(3, c, 0))
            self.wait(4, self.ref(3, c, 1))
            self.push(7, self.ref(3, c), self.ref(3, c), sibling)

        def pair(self):
            self.wait(2, self.ref(0, 1 - c))

        def near_pair(self):
            self.wait(5, self.ref(1, 1 - c))
            self.wait(6, self.ref(2, 1 - c))

        def far_pair(self):
            self.wait(7, self.ref(3, 1 - c))

    gx = [Gather(xg, 0, ch) for ch in range(3)]
    gw = [Gather(wg, 1, ch) for ch in range(3)]

    def share(ch):
        in_wait(ch)
        if ch == 2:
            in_wait(3)
        gx[ch].ref(0, c)[...] = bf16(dot(sel[...], a2a[:, lanes(ch)]))
        gx[ch].start()

    def gram(lo, hi):
        while lo < hi:
            n = min(384, hi - lo)
            gp[:, lo:lo + n] = bf16(dot(a2a[...], xg[lo:lo + n, :], ((1,), (1,))))
            lo += n

    def at(q):
        return slice(STRIPS[q][0], STRIPS[q][0] + STRIPS[q][1])

    def rs_send(q, k, d):
        t = block(y + signs[d] * (4 - k))
        send(gp.at[t, at(q)], rb.at[d, k, :, at(q)], rs_s.at[q, d, k], rs_r.at[q, d, k], ways[d])

    def rs_wait(q, k, d):
        arrive(rb.at[d, k, :, at(q)], rs_s.at[q, d, k], rs_r.at[q, d, k], ways[d])

    def rs_start(*strips):
        for q in strips:
            far = STRIPS[q][2]
            rs_send(q, 0, far)
            rs_send(q, 1, 1 - far)

    def rs_step(k, *strips):
        for q in strips:
            for d in range(2):
                if k == 1 and d != STRIPS[q][2]:
                    continue
                t = block(y + signs[d] * (4 - k))
                rs_wait(q, k - 1, d)
                gp[t, at(q)] = bf16(f32(gp[t, at(q)]) + f32(rb[d, k - 1, :, at(q)]))
                rs_send(q, k, d)

    def rs_end(*strips):
        for q in strips:
            rs_wait(q, 3, 0)
            rs_wait(q, 3, 1)
            zs[:, at(q)] = bf16(f32(gp[block(y), at(q)]) + f32(rb[0, 3, :, at(q)]) + f32(rb[1, 3, :, at(q)]))
            send(zs.at[:, at(q)], zr.at[:, at(q)], z_s.at[q], z_r.at[q], other_z)

    def gg_ref(q, k, d):
        return gf.at[block(y + (NY - signs[d]) * k), at(q)]

    def gg_send(q, k, d):
        send(gg_ref(q, k, d), gg_ref(q, k, d), gg_s.at[q, d, k], gg_r.at[q, d, k], ways[d])

    def gg_wait(q, k, d):
        arrive(gg_ref(q, k + 1, d), gg_s.at[q, d, k], gg_r.at[q, d, k], ways[d])

    def gg_start(*strips):
        for q in strips:
            arrive(zr.at[:, at(q)], z_s.at[q], z_r.at[q], other_z)
            gf[block(y), at(q)] = bf16(f32(zs[:, at(q)]) + f32(zr[:, at(q)]))
            for d in range(2):
                gg_send(q, 0, d)

    def gg_step(k, *strips):
        for q in strips:
            for d in range(2):
                gg_wait(q, k - 1, d)
                if k < 3 or d == STRIPS[q][2]:
                    gg_send(q, k, d)

    def gg_end(*strips):
        for q in strips:
            gg_wait(q, 3, STRIPS[q][2])

    share(0)
    share(1)
    gx[0].near()
    share(2)
    for g in gx:
        g.pair()
    gram(0, 640)
    rs_start(0, 1)
    gx[1].near()
    rs_step(1, 0, 1)
    gx[2].near()
    rs_step(2, 0, 1)
    for g in gx:
        g.near_pair()
    gram(640, 1920)
    rs_start(2, 3)
    rs_step(3, 0, 1)
    for g in gx:
        g.far()
    for g in gx:
        g.far_pair()
    gram(1920, 2688)
    rs_start(4, 5)
    rs_end(0, 1)
    rs_step(1, 2, 3, 4, 5)
    gg_start(0, 1)
    rs_step(2, 2, 3, 4, 5)
    gg_step(1, 0, 1)
    rs_step(3, 2, 3, 4, 5)
    gg_step(2, 0, 1)
    rs_end(2, 3, 4, 5)
    gg_step(3, 0, 1)
    gg_start(2, 3, 4, 5)
    gg_step(1, 2, 3, 4, 5)
    gg_step(2, 2, 3, 4, 5)
    gg_step(3, 2, 3, 4, 5)
    gg_end(0, 1, 2, 3, 4, 5)

    for ch in range(3):
        inner = cubic_term * f32(a2a[:, lanes(ch)]) + quintic_term * dot(gf[...], xg[:, lanes(ch)])
        gw[ch].ref(0, c)[...] = bf16(dot(sel[...], bf16(inner)))
        gw[ch].start()

    def out_copy(i, k, src, dst):
        off, size = CUTS[i]
        return copy(yp.at[block(dst), off:off + size], cut(y_ref, src, i),
                    out_s.at[i, k - 1], out_r.at[i, k - 1], ydev[k])

    drain()
    for g in gw:
        g.near()
    for ch in range(3):
        gw[ch].far()
        gw[ch].pair()
        gw[ch].near_pair()
        gw[ch].far_pair()
        yp[:, lanes(ch)] = bf16(dot(gf[...], wg[:, lanes(ch)]))
        for i in ((0,), (1,), (2, 3))[ch]:
            for k in ORDER:
                launch(out_copy(i, k, y, y + k), i, y)

            def own(i=i):
                cut(y_ref, y, i)[...] = yp[block(y), CUTS[i][0]:CUTS[i][0] + CUTS[i][1]]
            when_whole(i, y, own)

    for i in range(4):
        for k in ORDER:
            src = (y - k + NY) % NY
            when_whole(i, src, out_copy(i, k, src, y).wait_recv)
    drain()


def on_device(iterate):
    bf = jnp.bfloat16
    dma = pltpu.SemaphoreType.DMA
    local = iterate.shape[1]
    n = len(STRIPS)
    applied = pl.pallas_call(
        kernel,
        out_shape=jax.ShapeDtypeStruct((PAD, local), bf),
        in_specs=[pl.BlockSpec(memory_space=pl.ANY)],
        out_specs=pl.BlockSpec(memory_space=pltpu.VMEM),
        scratch_shapes=[
            pltpu.VMEM((OWN, local), jnp.float32),
            pltpu.VMEM((PAD, local), bf),
            pltpu.VMEM((DENSE, TALL), bf),
            pltpu.VMEM((TALL, WIDE), bf),
            pltpu.VMEM((FULL, WIDE), bf),
            pltpu.VMEM((FULL, WIDE), bf),
            pltpu.VMEM((TALL, FULL), bf),
            pltpu.VMEM((2, 4, PAD, FULL), bf),
            pltpu.VMEM((PAD, FULL), bf),
            pltpu.VMEM((PAD, FULL), bf),
            pltpu.VMEM((TALL, FULL), bf),
            pltpu.VMEM((TALL, WIDE), bf),
            dma,
            dma((4, 7)), dma((4, 7)),
            dma((2, 3, 8)), dma((2, 3, 8)),
            dma((n, 2, 4)), dma((n, 2, 4)),
            dma((n,)), dma((n,)),
            dma((n, 2, 4)), dma((n, 2, 4)),
            dma((4, 7)), dma((4, 7)),
        ],
        compiler_params=pltpu.CompilerParams(
            collective_id=0, has_side_effects=True, vmem_limit_bytes=50 * 2**20),
        name="newton_schulz",
    )(iterate)
    rounded = f32(iterate.astype(bf))
    return math.sqrt(COLS) * (linear_term * rounded + f32(applied[:OWN]))


def solution(mesh):
    spec = P(("mat", "row"), "col")
    return jax.shard_map(on_device, mesh=mesh, in_specs=(spec,), out_specs=spec, check_vma=False)
```

```python
import math

import jax
import jax.numpy as jnp
from jax import lax
from jax.experimental import pallas as pl
from jax.experimental.pallas import tpu as pltpu
from jax.sharding import PartitionSpec as P

COLS = 10752

linear_term = 3.4445
cubic_term = -4.775
quintic_term = 2.0315

NY = 8
NX = 4
NP = 8
OWN = 42
PAD = 48
DENSE = NY * OWN
SLOT = NY * PAD
WIDE = 768
CUTS = ((0, 128), (128, 256), (384, 256), (640, 128))
ORDER = (4, 3, 5, 2, 6, 1, 7)
UP, DOWN_PAIR, FAR, DOWN, UP_PAIR = 2, 3, 4, 5, 6
BLOCKS = 5
SUM = BLOCKS * SLOT
STRIPS = (
    (0, 768, 0, 0, False),
    (768, 384, 1, 2, True),
    (1152, 384, 0, 3, True),
    (1536, 384, 1, 4, True),
)


def dot(a, b, dims=((1,), (0,))):
    return lax.dot_general(a, b, (dims, ((), ())), preferred_element_type=jnp.float32)


def f32(v):
    return v.astype(jnp.float32)


def bf16(v):
    return v.astype(jnp.bfloat16)


def kernel(x_ref, y_ref, xs, sel, unsel, eye, a2a, xg, wg, gp, rb, zs, zr, gf, mx, gl, yp,
           in_s, in_r, ag_s, ag_r, rs_s, rs_r, z_s, z_r, gg_s, gg_r, mx_s, mx_r, out_s, out_r):
    m, r, z = lax.axis_index("mat"), lax.axis_index("row"), lax.axis_index("col")
    y, p = r // NP, r % NP
    x, c = p // 2, p % 2
    pending = []

    def dev(yy, xx, cc):
        return (m, (yy % NY) * NP + (xx % NX) * 2 + cc, z)

    def copy(src, dst, ssem, rsem, to):
        return pltpu.make_async_remote_copy(
            src_ref=src, dst_ref=dst, send_sem=ssem, recv_sem=rsem,
            device_id=to, device_id_type=pl.DeviceIdType.MESH)

    def send(src, dst, ssem, rsem, to):
        copy(src, dst, ssem, rsem, to).start()

    def arrive(ref, rsem):
        copy(ref, ref, rsem, rsem, sibling).wait_recv()

    def leave(ref, ssem):
        pending.append(copy(ref, ref, ssem, ssem, sibling).wait_send)

    def when_whole(i, yy, run):
        if i < 3:
            run()
        else:
            pl.when(yy % 4 == 3)(run)

    def whole(i, width, buf, act):
        if i < 3:
            act(buf.at[0:(NY - 1) * PAD, 0:width])()
        else:
            pl.when(y % 4 == 3)(act(buf.at[0:PAD, 0:width]))
            pl.when(y % 4 != 3)(act(buf.at[0:2 * PAD, 0:width]))

    def one(i, width, buf, act):
        when_whole(i, y, act(buf.at[0:(NY - 1) * PAD, 0:width]))

    def drain():
        for wait in pending:
            wait()
        pending.clear()

    sibling = dev(y, x, 1 - c)
    east, west = dev(y, x + 1, c), dev(y, x + 3, c)
    other_z = (m, r, 1 - z)
    ydev = [dev(y + k, x, c) for k in range(NY)]
    ways = (ydev[1], ydev[NY - 1])
    signs = (1, NY - 1)
    far_core = (c + x // 2) % 2
    partners = (east, dev(y, x + 3, 1 - c), dev(y, x + 2, far_core))
    mirrors = (west, dev(y, x + 1, 1 - c), dev(y, x + 2, 1 - far_core))

    a2a[:, 640:768] = jnp.zeros((SLOT, 128), jnp.bfloat16)
    barrier = pltpu.get_barrier_semaphore()
    greet = ydev[1:] + [sibling, east, west, other_z, partners[1], partners[2], mirrors[1], mirrors[2]]
    for to in greet:
        pl.semaphore_signal(barrier, inc=1, device_id=to, device_id_type=pl.DeviceIdType.MESH)

    xs[32:48, :] = jnp.zeros((16, xs.shape[1]), jnp.bfloat16)
    xs[0:OWN, :] = bf16(x_ref[...])
    pl.semaphore_wait(barrier, len(greet))

    def first(yy):
        return pl.multiple_of((21 * yy) // 4 * 128, 128)

    def cut(ref, yy, i):
        off, size = CUTS[i]
        return ref.at[:, pl.ds(pl.multiple_of(first(yy) + off, 128), size)]

    def block(yy):
        return pl.ds(pl.multiple_of((yy % NY) * PAD, 16), PAD)

    def in_copy(i, k, src, dst):
        off, size = CUTS[i]
        return copy(cut(xs, src, i), a2a.at[block(dst), off:off + size],
                    in_s.at[i], in_r.at[i], ydev[k])

    for i in range(4):
        for k in ORDER:
            when_whole(i, (y + k) % NY, in_copy(i, k, (y + k) % NY, y).start)
        pending.append(lambda i=i: whole(i, CUTS[i][1], a2a, lambda ref: copy(ref, ref, in_s.at[i], in_s.at[i], sibling).wait_send))

    for i, (off, size) in enumerate(CUTS):
        def own(i=i, off=off, size=size):
            a2a[block(y), off:off + size] = cut(xs, y, i)[...]
        when_whole(i, y, own)

    row = lax.broadcasted_iota(jnp.int32, (SLOT, SLOT), 0)
    col = lax.broadcasted_iota(jnp.int32, (SLOT, SLOT), 1)

    def spread(v):
        place = v
        for k in range(1, NY):
            place = place + jnp.where(v >= OWN * k, PAD - OWN, 0)
        return jnp.where(v < DENSE, place, -1)
    sel[...] = bf16(jnp.where(col == spread(row), 1.0, 0.0))
    unsel[...] = bf16(jnp.where(row == spread(col), 1.0, 0.0))
    eye[...] = bf16(jnp.where(row == col, 1.0, 0.0))
    for s in range(NP):
        xg[s * SLOT + DENSE:(s + 1) * SLOT, :] = jnp.zeros((SLOT - DENSE, WIDE), jnp.bfloat16)
        wg[s * SLOT + DENSE:(s + 1) * SLOT, :] = jnp.zeros((SLOT - DENSE, WIDE), jnp.bfloat16)

    def in_wait(i):
        one(i, CUTS[i][1], a2a, lambda ref: copy(ref, ref, in_r.at[i], in_r.at[i], sibling).wait_recv)

    def lanes(ch):
        return slice(CUTS[ch][0], CUTS[ch][0] + CUTS[ch][1])

    class Gather:
        def __init__(self, buf, n, ch):
            self.buf, self.n, self.ch = buf, n, ch

        def ref(self, slot, part=None):
            lo, size = ((0, DENSE), (0, 176), (176, 160))[0 if part is None else part + 1]
            return self.buf.at[pl.ds(pl.multiple_of(slot * SLOT + lo, 16), size), lanes(self.ch)]

        def far(self, xx):
            return FAR + 3 * ((xx % NX) // 2)

        def push(self, q, src, dst, to):
            rsem = ag_r.at[self.n, 0 if q > 2 and self.n == 0 else self.ch, q]
            send(src, dst, ag_s.at[self.n, self.ch], rsem, to)

        def wait(self, q, ref):
            arrive(ref, ag_r.at[self.n, self.ch, q])

        def start(self):
            mine = self.ref(c)
            self.push(0, mine, self.ref(DOWN), east)
            self.push(1, mine, self.ref(UP), west)
            self.push(3, mine, mine, sibling)
            if self.ch == 3:
                self.push(2, mine, self.ref(self.far(x + 2)), dev(y, x + 2, c))

        def near(self):
            self.wait(0, self.ref(DOWN))
            if self.ch < 3:
                self.push(2, self.ref(DOWN, 0), self.ref(self.far(x + 1), 0), east)
            self.push(4, self.ref(DOWN), self.ref(DOWN_PAIR), sibling)
            self.wait(1, self.ref(UP))
            if self.ch < 3:
                self.push(2, self.ref(UP, 1), self.ref(self.far(x + 3), 1), west)
            self.push(4, self.ref(UP), self.ref(UP_PAIR), sibling)

        def beyond(self):
            self.wait(2, self.ref(self.far(x)))
            self.push(5, self.ref(self.far(x)), self.ref(2 * FAR + 3 - self.far(x)), sibling)
            leave(self.buf.at[0:7 * DENSE, lanes(self.ch)], ag_s.at[self.n, self.ch])

        def pairs(self):
            for q, rows in ((3, 1), (4, 2), (5, 1)):
                self.wait(q, self.buf.at[0:rows * DENSE, lanes(self.ch)])

    gx = [Gather(xg, 0, ch) for ch in range(4)]
    gw = [Gather(wg, 1, ch) for ch in range(4)]

    def pairs(q):
        arrive(xg.at[0:(2 if q == 4 else 1) * DENSE, :], ag_r.at[0, 0, q])

    def mine(buf, ch):
        return buf.at[pl.ds(pl.multiple_of(c * SLOT, 16), SLOT), lanes(ch)]

    def share(ch):
        in_wait(ch)
        mine(xg, ch)[...] = bf16(dot(sel[...], a2a[:, lanes(ch)]))
        gx[ch].start()

    def gram(b):
        at = slice(b * SLOT, (b + 1) * SLOT)
        gp[:, at] = bf16(dot(a2a[...], xg[at, :], ((1,), (1,))))

    def at(q):
        return slice(STRIPS[q][0], STRIPS[q][0] + STRIPS[q][1])

    def rs_send(q, slot, t, k, to):
        send(gp.at[block(t), at(q)], rb.at[slot, :, at(q)], rs_s.at[q], rs_r.at[q, k], to)

    def rs_wait(q, k, n):
        arrive(rb.at[0:n, :, at(q)], rs_r.at[q, k])

    def add(t, q, *slots):
        v = f32(gp[block(t), at(q)])
        for slot in slots:
            v = v + f32(rb[slot, :, at(q)])
        return bf16(v)

    def rs_start(q):
        far = STRIPS[q][2]
        leave(gp.at[0:(NY - 1) * PAD, at(q)], rs_s.at[q])
        if STRIPS[q][4]:
            rs_send(q, 0, y + signs[far] * 4, 0, ydev[2 * signs[far] % NY])
            for d in range(2):
                rs_send(q, 1 + d, y + signs[d] * 3, 0, ways[d])
            for d in range(2):
                rs_send(q, 5 + d, y + signs[d], 1, ways[d])
        else:
            rs_send(q, 4 * far, y + 4, 0, ways[far])
            rs_send(q, 4 * (1 - far) + 1, y + signs[1 - far] * 3, 1, ways[1 - far])

    def rs_step(q, k):
        far = STRIPS[q][2]
        if STRIPS[q][4]:
            rs_wait(q, 0, 3)
            for d in (far, 1 - far):
                t = y + signs[d] * 2
                gp[block(t), at(q)] = add(t, q, 1 + d, 0) if d == far else add(t, q, 1 + d)
                rs_send(q, 3 + d, t, 1, ydev[2 * signs[d] % NY])
            return
        rs_wait(q, k - 1, 1 if k == 1 else 2)
        for d in range(2):
            if k == 1 and d != far:
                continue
            t = y + signs[d] * (4 - k)
            gp[block(t), at(q)] = add(t, q, 4 * d + k - 1)
            rs_send(q, 4 * d + k, t, k, ways[d])

    def rs_end(q):
        if STRIPS[q][4]:
            rs_wait(q, 1, 4)
            zs[:, at(q)] = add(y, q, 3, 4, 5, 6)
        else:
            rs_wait(q, 3, 2)
            zs[:, at(q)] = add(y, q, 3, 7)
        send(zs.at[:, at(q)], zr.at[:, at(q)], z_s.at[q], z_r.at[q], other_z)
        leave(zs.at[:, at(q)], z_s.at[q])

    def mirror(q, j):
        b = STRIPS[q][3] - UP
        if b >= 0:
            send(gf.at[block(y + j), at(q)], mx.at[b, block(y + j), :], mx_s.at[b], mx_r.at[b], partners[b])

    def gg_send(q, j, k, to):
        ref = gf.at[block(y + j), at(q)]
        send(ref, ref, gg_s.at[q], gg_r.at[q, k], to)

    def gg_wait(q, k, n):
        arrive(gf.at[0:n * PAD, at(q)], gg_r.at[q, k])

    def gg_start(q):
        arrive(zr.at[:, at(q)], z_r.at[q])
        gf[block(y), at(q)] = bf16(f32(zs[:, at(q)]) + f32(zr[:, at(q)]))
        leave(gf.at[0:(NY - 1) * PAD, at(q)], gg_s.at[q])
        for d in range(2):
            if STRIPS[q][4]:
                gg_send(q, 0, 0, ydev[2 * signs[d] % NY])
            gg_send(q, 0, 0, ways[d])
        mirror(q, 0)
        if STRIPS[q][3] >= UP:
            b = STRIPS[q][3] - UP
            leave(gf.at[:, at(q)], mx_s.at[b])

    def gg_step(q, k):
        far = STRIPS[q][2]
        if STRIPS[q][4]:
            gg_wait(q, 0, 4)
            for d in range(2):
                back = NY - signs[d] * 2 % NY
                if d == far:
                    gg_send(q, back, 1, ydev[2 * signs[d] % NY])
                gg_send(q, back, 1, ways[d])
            for j in (1, NY - 1, 2, NY - 2):
                mirror(q, j)
            return
        gg_wait(q, k - 1, 2)
        for d in range(2):
            back = NY - signs[d] * k % NY
            if k < 3 or d == far:
                gg_send(q, back, k, ways[d])
            mirror(q, back)

    def gg_end(q):
        if STRIPS[q][4]:
            gg_wait(q, 1, 3)
            for j in (3, NY - 3, 4):
                mirror(q, j)
        else:
            gg_wait(q, 3, 1)
            mirror(q, 4)

    def mirror_wait(b):
        arrive(mx.at[b], mx_r.at[b])

    def settle(b):
        at = slice(b * SLOT, (b + 1) * SLOT)
        if b < BLOCKS:
            gl[:, at] = bf16(dot(sel[...], gf[:, at]))
        else:
            turned = bf16(dot(eye[...], mx[b - BLOCKS], ((1,), (1,))))
            gl[:, at] = bf16(dot(turned, sel[...], ((1,), (1,))))

    A, B, C, D = range(4)
    share(0)
    share(1)
    gx[0].near()
    share(2)
    gx[1].near()
    share(3)
    pairs(3)
    gram(0)
    gram(1)
    rs_start(A)
    gx[2].near()
    gx[0].beyond()
    rs_step(A, 1)
    gx[3].near()
    gram(2)
    rs_start(B)
    gx[1].beyond()
    rs_step(A, 2)
    pairs(4)
    gram(3)
    rs_start(C)
    gx[2].beyond()
    gx[3].beyond()
    rs_step(A, 3)
    rs_step(B, 1)
    pairs(5)
    gram(4)
    rs_start(D)
    rs_step(C, 1)
    rs_end(A)
    rs_end(B)
    rs_step(D, 1)
    gg_start(A)
    rs_end(C)
    gg_start(B)
    rs_end(D)
    gg_step(A, 1)
    gg_start(C)
    gg_step(B, 1)
    gg_start(D)
    gg_step(A, 2)
    gg_step(C, 1)
    gg_end(B)
    gg_step(D, 1)
    gg_step(A, 3)
    settle(2)
    gg_end(C)
    settle(3)
    gg_end(D)
    gg_end(A)
    settle(4)
    settle(0)
    settle(1)
    for b in range(3):
        mirror_wait(b)
        settle(BLOCKS + b)

    def inner(ch):
        v = cubic_term * f32(mine(xg, ch)[...]) + quintic_term * dot(gl[...], xg[:, lanes(ch)])
        mine(wg, ch)[...] = bf16(v)
        gw[ch].start()

    def out_copy(i, k, src, dst):
        off, size = CUTS[i]
        return copy(yp.at[block(dst), off:off + size], cut(y_ref, src, i),
                    out_s.at[i], out_r.at[i], ydev[k])

    def outer(ch):
        gw[ch].pairs()
        yp[:, lanes(ch)] = bf16(dot(unsel[...], bf16(dot(gl[...], wg[:, lanes(ch)]))))
        for k in ORDER:
            when_whole(ch, y, out_copy(ch, k, y, y + k).start)
        pending.append(lambda: one(ch, CUTS[ch][1], yp, lambda ref: copy(ref, ref, out_s.at[ch], out_s.at[ch], sibling).wait_send))

        def own():
            cut(y_ref, y, ch)[...] = yp[block(y), lanes(ch)]
        when_whole(ch, y, own)

    inner(0)
    inner(1)
    drain()
    gw[0].near()
    inner(2)
    gw[1].near()
    gw[0].beyond()
    inner(3)
    gw[2].near()
    outer(0)
    gw[1].beyond()
    gw[3].near()
    outer(1)
    gw[2].beyond()
    gw[3].beyond()
    outer(2)
    outer(3)
    for i in range(4):
        whole(i, CUTS[i][1], yp, lambda ref: copy(ref, ref, out_r.at[i], out_r.at[i], sibling).wait_recv)
    drain()


def on_device(iterate):
    bf = jnp.bfloat16
    dma = pltpu.SemaphoreType.DMA
    local = iterate.shape[1]
    n = len(STRIPS)
    applied = pl.pallas_call(
        kernel,
        out_shape=jax.ShapeDtypeStruct((PAD, local), bf),
        in_specs=[pl.BlockSpec(memory_space=pltpu.VMEM)],
        out_specs=pl.BlockSpec(memory_space=pltpu.VMEM),
        scratch_shapes=[
            pltpu.VMEM((PAD, local), bf),
            pltpu.VMEM((SLOT, SLOT), bf),
            pltpu.VMEM((SLOT, SLOT), bf),
            pltpu.VMEM((SLOT, SLOT), bf),
            pltpu.VMEM((SLOT, WIDE), bf),
            pltpu.VMEM((NP * SLOT, WIDE), bf),
            pltpu.VMEM((NP * SLOT, WIDE), bf),
            pltpu.VMEM((SLOT, SUM), bf),
            pltpu.VMEM((8, PAD, SUM), bf),
            pltpu.VMEM((PAD, SUM), bf),
            pltpu.VMEM((PAD, SUM), bf),
            pltpu.VMEM((SLOT, SUM), bf),
            pltpu.VMEM((3, SLOT, SLOT), bf),
            pltpu.VMEM((SLOT, NP * SLOT), bf),
            pltpu.VMEM((SLOT, WIDE), bf),
            dma((4,)), dma((4,)),
            dma((2, 4)), dma((2, 4, 6)),
            dma((n,)), dma((n, 4)),
            dma((n,)), dma((n,)),
            dma((n,)), dma((n, 4)),
            dma((3,)), dma((3,)),
            dma((4,)), dma((4,)),
        ],
        compiler_params=pltpu.CompilerParams(
            collective_id=0, has_side_effects=True, vmem_limit_bytes=50 * 2**20),
        name="newton_schulz",
    )(iterate)
    rounded = f32(iterate.astype(bf))
    return math.sqrt(COLS) * (linear_term * rounded + f32(applied[:OWN]))


def solution(mesh):
    spec = P(("mat", "row"), "col")
    return jax.shard_map(on_device, mesh=mesh, in_specs=(spec,), out_specs=spec, check_vma=False)
```

```python
import math

import jax
import jax.numpy as jnp
from jax import lax
from jax.experimental import pallas as pl
from jax.experimental.pallas import tpu as pltpu
from jax.sharding import PartitionSpec as P

COLS = 10752

linear_term = 3.4445
cubic_term = -4.775
quintic_term = 2.0315

NY = 8
NX = 4
NP = 8
OWN = 42
PAD = 48
DENSE = NY * OWN
SLOT = NY * PAD
WIDE = 768
CUTS = ((0, 128), (128, 256), (384, 256), (640, 128))
ORDER = (4, 3, 5, 2, 6, 1, 7)
UP, DOWN_PAIR, FAR, DOWN, UP_PAIR = 2, 3, 4, 5, 6
BLOCKS = 5
SUM = BLOCKS * SLOT
STRIPS = (
    (0, 768, 0, 0, True),
    (768, 384, 1, 2, True),
    (1152, 384, 0, 3, True),
    (1536, 384, 1, 4, True),
)
GROUPS = ((0, 0, False, True), (768, 1, True, True), (1536, 1, True, False))


def dot(a, b, dims=((1,), (0,))):
    return lax.dot_general(a, b, (dims, ((), ())), preferred_element_type=jnp.float32)


def f32(v):
    return v.astype(jnp.float32)


def bf16(v):
    return v.astype(jnp.bfloat16)


def kernel(x_ref, y_ref, xs, sel, unsel, eye, a2a, xg, wg, gp, rb, zs, zr, gf, mx, gl, yp,
           in_s, in_r, ag_s, ag_r, rs_s, rs_r, z_s, z_r, gg_s, gg_r, zf_s, zf_r, mx_s, mx_r, out_s, out_r):
    m, r, z = lax.axis_index("mat"), lax.axis_index("row"), lax.axis_index("col")
    y, p = r // NP, r % NP
    x, c = p // 2, p % 2
    pending = []

    def dev(yy, xx, cc):
        return (m, (yy % NY) * NP + (xx % NX) * 2 + cc, z)

    def copy(src, dst, ssem, rsem, to):
        return pltpu.make_async_remote_copy(
            src_ref=src, dst_ref=dst, send_sem=ssem, recv_sem=rsem,
            device_id=to, device_id_type=pl.DeviceIdType.MESH)

    def send(src, dst, ssem, rsem, to):
        copy(src, dst, ssem, rsem, to).start()

    def arrive(ref, rsem):
        copy(ref, ref, rsem, rsem, sibling).wait_recv()

    def leave(ref, ssem):
        pending.append(copy(ref, ref, ssem, ssem, sibling).wait_send)

    def when_whole(i, yy, run):
        if i < 3:
            run()
        else:
            pl.when(yy % 4 == 3)(run)

    def whole(i, width, buf, act):
        if i < 3:
            act(buf.at[0:(NY - 1) * PAD, 0:width])()
        else:
            pl.when(y % 4 == 3)(act(buf.at[0:PAD, 0:width]))
            pl.when(y % 4 != 3)(act(buf.at[0:2 * PAD, 0:width]))

    def one(i, width, buf, act):
        when_whole(i, y, act(buf.at[0:(NY - 1) * PAD, 0:width]))

    def drain():
        for wait in pending:
            wait()
        pending.clear()

    sibling = dev(y, x, 1 - c)
    east, west = dev(y, x + 1, c), dev(y, x + 3, c)
    other_z = (m, r, 1 - z)
    ydev = [dev(y + k, x, c) for k in range(NY)]
    ways = (ydev[1], ydev[NY - 1])
    signs = (1, NY - 1)
    far_core = (c + x // 2) % 2
    partners = (east, dev(y, x + 3, 1 - c), dev(y, x + 2, far_core))
    mirrors = (west, dev(y, x + 1, 1 - c), dev(y, x + 2, 1 - far_core))

    a2a[:, 640:768] = jnp.zeros((SLOT, 128), jnp.bfloat16)
    barrier = pltpu.get_barrier_semaphore()
    greet = ydev[1:] + [sibling, east, west, other_z, partners[1], partners[2], mirrors[1], mirrors[2]]
    for to in greet:
        pl.semaphore_signal(barrier, inc=1, device_id=to, device_id_type=pl.DeviceIdType.MESH)

    xs[32:48, :] = jnp.zeros((16, xs.shape[1]), jnp.bfloat16)
    xs[0:OWN, :] = bf16(x_ref[...])
    pl.semaphore_wait(barrier, len(greet))

    def first(yy):
        return pl.multiple_of((21 * yy) // 4 * 128, 128)

    def cut(ref, yy, i):
        off, size = CUTS[i]
        return ref.at[:, pl.ds(pl.multiple_of(first(yy) + off, 128), size)]

    def block(yy):
        return pl.ds(pl.multiple_of((yy % NY) * PAD, 16), PAD)

    def in_copy(i, k, src, dst):
        off, size = CUTS[i]
        return copy(cut(xs, src, i), a2a.at[block(dst), off:off + size],
                    in_s.at[i], in_r.at[i], ydev[k])

    for i in range(4):
        for k in ORDER:
            when_whole(i, (y + k) % NY, in_copy(i, k, (y + k) % NY, y).start)
        pending.append(lambda i=i: whole(i, CUTS[i][1], a2a, lambda ref: copy(ref, ref, in_s.at[i], in_s.at[i], sibling).wait_send))

    for i, (off, size) in enumerate(CUTS):
        def own(i=i, off=off, size=size):
            a2a[block(y), off:off + size] = cut(xs, y, i)[...]
        when_whole(i, y, own)

    row = lax.broadcasted_iota(jnp.int32, (SLOT, SLOT), 0)
    col = lax.broadcasted_iota(jnp.int32, (SLOT, SLOT), 1)

    def spread(v):
        place = v
        for k in range(1, NY):
            place = place + jnp.where(v >= OWN * k, PAD - OWN, 0)
        return jnp.where(v < DENSE, place, -1)
    sel[...] = bf16(jnp.where(col == spread(row), 1.0, 0.0))
    unsel[...] = bf16(jnp.where(row == spread(col), 1.0, 0.0))
    eye[...] = bf16(jnp.where(row == col, 1.0, 0.0))
    for s in range(NP):
        xg[s * SLOT + DENSE:(s + 1) * SLOT, :] = jnp.zeros((SLOT - DENSE, WIDE), jnp.bfloat16)
        wg[s * SLOT + DENSE:(s + 1) * SLOT, :] = jnp.zeros((SLOT - DENSE, WIDE), jnp.bfloat16)

    def in_wait(i):
        one(i, CUTS[i][1], a2a, lambda ref: copy(ref, ref, in_r.at[i], in_r.at[i], sibling).wait_recv)

    def lanes(ch):
        return slice(CUTS[ch][0], CUTS[ch][0] + CUTS[ch][1])

    class Gather:
        def __init__(self, buf, n, ch):
            self.buf, self.n, self.ch = buf, n, ch

        def ref(self, slot, part=None):
            lo, size = ((0, DENSE), (0, 176), (176, 160))[0 if part is None else part + 1]
            return self.buf.at[pl.ds(pl.multiple_of(slot * SLOT + lo, 16), size), lanes(self.ch)]

        def far(self, xx):
            return FAR + 3 * ((xx % NX) // 2)

        def push(self, q, src, dst, to):
            rsem = ag_r.at[self.n, 0 if q > 2 and self.n == 0 else self.ch, q]
            send(src, dst, ag_s.at[self.n, self.ch], rsem, to)

        def wait(self, q, ref):
            arrive(ref, ag_r.at[self.n, self.ch, q])

        def start(self):
            mine = self.ref(c)
            self.push(0, mine, self.ref(DOWN), east)
            self.push(1, mine, self.ref(UP), west)
            self.push(3, mine, mine, sibling)
            if self.ch == 3:
                self.push(2, mine, self.ref(self.far(x + 2)), dev(y, x + 2, c))

        def near(self):
            self.wait(0, self.ref(DOWN))
            if self.ch < 3:
                self.push(2, self.ref(DOWN, 0), self.ref(self.far(x + 1), 0), east)
            self.push(4, self.ref(DOWN), self.ref(DOWN_PAIR), sibling)
            self.wait(1, self.ref(UP))
            if self.ch < 3:
                self.push(2, self.ref(UP, 1), self.ref(self.far(x + 3), 1), west)
            self.push(4, self.ref(UP), self.ref(UP_PAIR), sibling)

        def beyond(self):
            self.wait(2, self.ref(self.far(x)))
            self.push(5, self.ref(self.far(x)), self.ref(2 * FAR + 3 - self.far(x)), sibling)
            leave(self.buf.at[0:7 * DENSE, lanes(self.ch)], ag_s.at[self.n, self.ch])

        def pairs(self):
            for q, rows in ((3, 1), (4, 2), (5, 1)):
                self.wait(q, self.buf.at[0:rows * DENSE, lanes(self.ch)])

    gx = [Gather(xg, 0, ch) for ch in range(4)]
    gw = [Gather(wg, 1, ch) for ch in range(4)]

    def pairs(q):
        arrive(xg.at[0:(2 if q == 4 else 1) * DENSE, :], ag_r.at[0, 0, q])

    def mine(buf, ch):
        return buf.at[pl.ds(pl.multiple_of(c * SLOT, 16), SLOT), lanes(ch)]

    def share(ch):
        in_wait(ch)
        mine(xg, ch)[...] = bf16(dot(sel[...], a2a[:, lanes(ch)]))
        gx[ch].start()

    def gram(b):
        at = slice(b * SLOT, (b + 1) * SLOT)
        gp[:, at] = bf16(dot(a2a[...], xg[at, :], ((1,), (1,))))

    def at(q):
        return slice(STRIPS[q][0], STRIPS[q][0] + STRIPS[q][1])

    def rs_send(q, slot, t, k, to):
        send(gp.at[block(t), at(q)], rb.at[slot, :, at(q)], rs_s.at[q], rs_r.at[q, k], to)

    def rs_wait(q, k, n):
        arrive(rb.at[0:n, :, at(q)], rs_r.at[q, k])

    def add(t, q, *slots):
        v = f32(gp[block(t), at(q)])
        for slot in slots:
            v = v + f32(rb[slot, :, at(q)])
        return bf16(v)

    def rs_start(q):
        far = STRIPS[q][2]
        leave(gp.at[0:(NY - 1) * PAD, at(q)], rs_s.at[q])
        if STRIPS[q][4]:
            rs_send(q, 0, y + signs[far] * 4, 0, ydev[2 * signs[far] % NY])
            for d in range(2):
                rs_send(q, 1 + d, y + signs[d] * 3, 0, ways[d])
            for d in range(2):
                rs_send(q, 5 + d, y + signs[d], 1, ways[d])
        else:
            rs_send(q, 4 * far, y + 4, 0, ways[far])
            rs_send(q, 4 * (1 - far) + 1, y + signs[1 - far] * 3, 1, ways[1 - far])

    def rs_step(q, k):
        far = STRIPS[q][2]
        if STRIPS[q][4]:
            rs_wait(q, 0, 3)
            for d in (far, 1 - far):
                t = y + signs[d] * 2
                gp[block(t), at(q)] = add(t, q, 1 + d, 0) if d == far else add(t, q, 1 + d)
                rs_send(q, 3 + d, t, 1, ydev[2 * signs[d] % NY])
            return
        rs_wait(q, k - 1, 1 if k == 1 else 2)
        for d in range(2):
            if k == 1 and d != far:
                continue
            t = y + signs[d] * (4 - k)
            gp[block(t), at(q)] = add(t, q, 4 * d + k - 1)
            rs_send(q, 4 * d + k, t, k, ways[d])

    def rs_end(q):
        if STRIPS[q][4]:
            rs_wait(q, 1, 4)
            zs[:, at(q)] = add(y, q, 3, 4, 5, 6)
        else:
            rs_wait(q, 3, 2)
            zs[:, at(q)] = add(y, q, 3, 7)

    def gat(g, side):
        lo, _, _, shared = GROUPS[g]
        return pl.ds(pl.multiple_of(lo + side * SLOT, 128), SLOT) if shared else slice(lo, lo + SLOT)

    def z_send(g):
        theirs = gat(g, 1 - z)
        send(zs.at[:, theirs], zr.at[:, theirs], z_s.at[g], z_r.at[g], other_z)
        leave(zs.at[:, 0:SLOT], z_s.at[g])

    def mirror(g, j, side):
        ref = gf.at[block(y + j), gat(g, side)]
        if g == 1:
            i = (side - z) % 2
            send(ref, mx.at[side, block(y + j), :], mx_s.at[i], mx_r.at[i], dev(y, x + 1 + 2 * side, (c + side) % 2))
        elif g == 2:
            send(ref, mx.at[2, block(y + j), :], mx_s.at[2], mx_r.at[2], partners[2])

    def spread_on(g, k, *js):
        for j in js:
            if GROUPS[g][3]:
                ref = gf.at[block(y + j), gat(g, z)]
                send(ref, ref, zf_s.at[g], zf_r.at[g, k], other_z)
            mirror(g, j, z)

    def zf_wait(g, k, *js):
        arrive(gf.at[0:len(js) * PAD, 0:SLOT], zf_r.at[g, k])
        for j in js:
            mirror(g, j, 1 - z)

    def gg_send(g, j, k, to):
        ref = gf.at[block(y + j), gat(g, z)]
        send(ref, ref, gg_s.at[g], gg_r.at[g, k], to)

    def gg_wait(g, k, n):
        arrive(gf.at[0:n * PAD, 0:SLOT], gg_r.at[g, k])

    def gg_start(g):
        here = gat(g, z)
        arrive(zr.at[:, 0:SLOT], z_r.at[g])
        gf[block(y), here] = bf16(f32(zs[:, here]) + f32(zr[:, here]))
        leave(gf.at[0:(NY - 1) * PAD, 0:SLOT], gg_s.at[g])
        for d in range(2):
            if GROUPS[g][2]:
                gg_send(g, 0, 0, ydev[2 * signs[d] % NY])
            gg_send(g, 0, 0, ways[d])
        spread_on(g, 0, 0)
        if GROUPS[g][3]:
            leave(gf.at[:, 0:SLOT], zf_s.at[g])
        if g == 1:
            leave(gf.at[:, 0:SLOT], mx_s.at[0])
            leave(gf.at[:, 0:SLOT], mx_s.at[1])
        elif g == 2:
            leave(gf.at[:, 0:SLOT], mx_s.at[2])

    def gg_step(g, k):
        far = GROUPS[g][1]
        if GROUPS[g][2]:
            gg_wait(g, 0, 4)
            for d in range(2):
                back = NY - signs[d] * 2 % NY
                if d == far:
                    gg_send(g, back, 1, ydev[2 * signs[d] % NY])
                gg_send(g, back, 1, ways[d])
            spread_on(g, 0, 1, NY - 1, 2, NY - 2)
            return
        gg_wait(g, k - 1, 2)
        for d in range(2):
            back = NY - signs[d] * k % NY
            if k < 3 or d == far:
                gg_send(g, back, k, ways[d])
            spread_on(g, 0, back)

    def gg_end(g):
        if GROUPS[g][2]:
            gg_wait(g, 1, 3)
            spread_on(g, 1, 3, NY - 3, 4)
        else:
            gg_wait(g, 3, 1)
            spread_on(g, 0, 4)

    def mirror_wait(b):
        arrive(mx.at[b], mx_r.at[b])

    def settle(b):
        at = slice(b * SLOT, (b + 1) * SLOT)
        if b < BLOCKS:
            gl[:, at] = bf16(dot(sel[...], gf[:, at]))
        else:
            turned = bf16(dot(eye[...], mx[b - BLOCKS], ((1,), (1,))))
            gl[:, at] = bf16(dot(turned, sel[...], ((1,), (1,))))

    A, B, C, D = range(4)
    share(0)
    share(1)
    share(2)
    gx[0].near()
    share(3)
    gx[1].near()
    pairs(3)
    gram(0)
    gram(1)
    rs_start(A)
    gx[2].near()
    gx[0].beyond()
    gx[3].near()
    gram(2)
    rs_start(B)
    rs_step(A, 1)
    gx[1].beyond()
    pairs(4)
    gram(3)
    rs_start(C)
    gx[2].beyond()
    gx[3].beyond()
    rs_end(A)
    z_send(0)
    rs_step(B, 1)
    pairs(5)
    gram(4)
    rs_start(D)
    rs_step(C, 1)
    gg_start(0)
    rs_end(B)
    rs_step(D, 1)
    rs_end(C)
    z_send(1)
    gg_step(0, 1)
    rs_end(D)
    z_send(2)
    gg_start(1)
    gg_step(0, 2)
    gg_start(2)
    gg_step(0, 3)
    gg_step(1, 1)
    gg_end(0)
    gg_step(2, 1)
    gg_end(1)
    zf_wait(1, 0, 0, 1, NY - 1, 2, NY - 2)
    gg_end(2)
    zf_wait(1, 1, 3, NY - 3, 4)
    settle(4)
    zf_wait(0, 0, *range(NY))
    for b in range(4):
        settle(b)
    mirror_wait(2)
    settle(7)
    mirror_wait(0)
    mirror_wait(1)
    settle(5)
    settle(6)

    def inner(ch):
        v = cubic_term * f32(mine(xg, ch)[...]) + quintic_term * dot(gl[...], xg[:, lanes(ch)])
        mine(wg, ch)[...] = bf16(v)
        gw[ch].start()

    def out_copy(i, k, src, dst):
        off, size = CUTS[i]
        return copy(yp.at[block(dst), off:off + size], cut(y_ref, src, i),
                    out_s.at[i], out_r.at[i], ydev[k])

    def outer(ch):
        gw[ch].pairs()
        yp[:, lanes(ch)] = bf16(dot(unsel[...], bf16(dot(gl[...], wg[:, lanes(ch)]))))
        for k in ORDER:
            when_whole(ch, y, out_copy(ch, k, y, y + k).start)
        pending.append(lambda: one(ch, CUTS[ch][1], yp, lambda ref: copy(ref, ref, out_s.at[ch], out_s.at[ch], sibling).wait_send))

        def own():
            cut(y_ref, y, ch)[...] = yp[block(y), lanes(ch)]
        when_whole(ch, y, own)

    inner(0)
    inner(1)
    drain()
    gw[0].near()
    inner(2)
    gw[1].near()
    gw[0].beyond()
    inner(3)
    outer(0)
    gw[2].near()
    gw[1].beyond()
    gw[3].near()
    outer(1)
    gw[2].beyond()
    gw[3].beyond()
    outer(2)
    outer(3)
    for i in range(4):
        whole(i, CUTS[i][1], yp, lambda ref: copy(ref, ref, out_r.at[i], out_r.at[i], sibling).wait_recv)
    drain()


def on_device(iterate):
    bf = jnp.bfloat16
    dma = pltpu.SemaphoreType.DMA
    local = iterate.shape[1]
    n = len(STRIPS)
    applied = pl.pallas_call(
        kernel,
        out_shape=jax.ShapeDtypeStruct((PAD, local), bf),
        in_specs=[pl.BlockSpec(memory_space=pltpu.VMEM)],
        out_specs=pl.BlockSpec(memory_space=pltpu.VMEM),
        scratch_shapes=[
            pltpu.VMEM((PAD, local), bf),
            pltpu.VMEM((SLOT, SLOT), bf),
            pltpu.VMEM((SLOT, SLOT), bf),
            pltpu.VMEM((SLOT, SLOT), bf),
            pltpu.VMEM((SLOT, WIDE), bf),
            pltpu.VMEM((NP * SLOT, WIDE), bf),
            pltpu.VMEM((NP * SLOT, WIDE), bf),
            pltpu.VMEM((SLOT, SUM), bf),
            pltpu.VMEM((8, PAD, SUM), bf),
            pltpu.VMEM((PAD, SUM), bf),
            pltpu.VMEM((PAD, SUM), bf),
            pltpu.VMEM((SLOT, SUM), bf),
            pltpu.VMEM((3, SLOT, SLOT), bf),
            pltpu.VMEM((SLOT, NP * SLOT), bf),
            pltpu.VMEM((SLOT, WIDE), bf),
            dma((4,)), dma((4,)),
            dma((2, 4)), dma((2, 4, 6)),
            dma((n,)), dma((n, 4)),
            dma((3,)), dma((3,)),
            dma((3,)), dma((3, 4)),
            dma((2,)), dma((2, 2)),
            dma((3,)), dma((3,)),
            dma((4,)), dma((4,)),
        ],
        compiler_params=pltpu.CompilerParams(
            collective_id=0, has_side_effects=True, vmem_limit_bytes=50 * 2**20),
        name="newton_schulz",
    )(iterate)
    rounded = f32(iterate.astype(bf))
    return math.sqrt(COLS) * (linear_term * rounded + f32(applied[:OWN]))


def solution(mesh):
    spec = P(("mat", "row"), "col")
    return jax.shard_map(on_device, mesh=mesh, in_specs=(spec,), out_specs=spec, check_vma=False)
```

```python
import math

import jax
import jax.numpy as jnp
from jax import lax
from jax.experimental import pallas as pl
from jax.experimental.pallas import tpu as pltpu
from jax.sharding import PartitionSpec as P

COLS = 10752

linear_term = 3.4445
cubic_term = -4.775
quintic_term = 2.0315

NY = 8
NX = 4
NP = 8
OWN = 42
PAD = 48
DENSE = NY * OWN
SLOT = NY * PAD
WIDE = 768
CUTS = ((0, 128), (128, 256), (384, 256), (640, 128))
ORDER = (4, 3, 5, 2, 6, 1, 7)
UP, DOWN_PAIR, FAR, DOWN, UP_PAIR = 2, 3, 4, 5, 6
BLOCKS = 5
SUM = BLOCKS * SLOT
STRIPS = (
    (0, 768, 0, 0, True),
    (768, 384, 1, 2, True),
    (1152, 384, 0, 3, True),
    (1536, 384, 1, 4, True),
)
GROUPS = ((0, 0, False, True), (768, 1, True, False), (1536, 1, True, False), (1152, 0, True, False))


def dot(a, b, dims=((1,), (0,))):
    return lax.dot_general(a, b, (dims, ((), ())), preferred_element_type=jnp.float32)


def f32(v):
    return v.astype(jnp.float32)


def bf16(v):
    return v.astype(jnp.bfloat16)


def kernel(x_ref, y_ref, xs, sel, unsel, eye, a2a, xg, wg, gp, rb, zs, zr, gf, mx, gl, yp,
           in_s, in_r, ag_s, ag_r, rs_s, rs_r, z_s, z_r, gg_s, gg_r, zf_s, zf_r, mx_s, mx_r, out_s, out_r):
    m, r, z = lax.axis_index("mat"), lax.axis_index("row"), lax.axis_index("col")
    y, p = r // NP, r % NP
    x, c = p // 2, p % 2
    pending = []

    def dev(yy, xx, cc):
        return (m, (yy % NY) * NP + (xx % NX) * 2 + cc, z)

    def copy(src, dst, ssem, rsem, to):
        return pltpu.make_async_remote_copy(
            src_ref=src, dst_ref=dst, send_sem=ssem, recv_sem=rsem,
            device_id=to, device_id_type=pl.DeviceIdType.MESH)

    def send(src, dst, ssem, rsem, to):
        copy(src, dst, ssem, rsem, to).start()

    def arrive(ref, rsem):
        copy(ref, ref, rsem, rsem, sibling).wait_recv()

    def leave(ref, ssem):
        pending.append(copy(ref, ref, ssem, ssem, sibling).wait_send)

    def when_whole(i, yy, run):
        if i < 3:
            run()
        else:
            pl.when(yy % 4 == 3)(run)

    def whole(i, width, buf, act):
        if i < 3:
            act(buf.at[0:(NY - 1) * PAD, 0:width])()
        else:
            pl.when(y % 4 == 3)(act(buf.at[0:PAD, 0:width]))
            pl.when(y % 4 != 3)(act(buf.at[0:2 * PAD, 0:width]))

    def one(i, width, buf, act):
        when_whole(i, y, act(buf.at[0:(NY - 1) * PAD, 0:width]))

    def drain():
        for wait in pending:
            wait()
        pending.clear()

    sibling = dev(y, x, 1 - c)
    east, west = dev(y, x + 1, c), dev(y, x + 3, c)
    other_z = (m, r, 1 - z)
    ydev = [dev(y + k, x, c) for k in range(NY)]
    ways = (ydev[1], ydev[NY - 1])
    signs = (1, NY - 1)
    far_core = (c + x // 2) % 2
    partners = (east, dev(y, x + 3, 1 - c), dev(y, x + 2, far_core))
    mirrors = (west, dev(y, x + 1, 1 - c), dev(y, x + 2, 1 - far_core))

    a2a[:, 640:768] = jnp.zeros((SLOT, 128), jnp.bfloat16)
    barrier = pltpu.get_barrier_semaphore()
    greet = ydev[1:] + [sibling, east, west, other_z, partners[1], partners[2], mirrors[1], mirrors[2]]
    for to in greet:
        pl.semaphore_signal(barrier, inc=1, device_id=to, device_id_type=pl.DeviceIdType.MESH)

    xs[32:48, :] = jnp.zeros((16, xs.shape[1]), jnp.bfloat16)
    xs[0:OWN, :] = bf16(x_ref[...])
    pl.semaphore_wait(barrier, len(greet))

    def first(yy):
        return pl.multiple_of((21 * yy) // 4 * 128, 128)

    def cut(ref, yy, i):
        off, size = CUTS[i]
        return ref.at[:, pl.ds(pl.multiple_of(first(yy) + off, 128), size)]

    def block(yy):
        return pl.ds(pl.multiple_of((yy % NY) * PAD, 16), PAD)

    def in_copy(i, k, src, dst):
        off, size = CUTS[i]
        return copy(cut(xs, src, i), a2a.at[block(dst), off:off + size],
                    in_s.at[i], in_r.at[i], ydev[k])

    for i in range(4):
        for k in ORDER:
            when_whole(i, (y + k) % NY, in_copy(i, k, (y + k) % NY, y).start)
        pending.append(lambda i=i: whole(i, CUTS[i][1], a2a, lambda ref: copy(ref, ref, in_s.at[i], in_s.at[i], sibling).wait_send))

    for i, (off, size) in enumerate(CUTS):
        def own(i=i, off=off, size=size):
            a2a[block(y), off:off + size] = cut(xs, y, i)[...]
        when_whole(i, y, own)

    row = lax.broadcasted_iota(jnp.int32, (SLOT, SLOT), 0)
    col = lax.broadcasted_iota(jnp.int32, (SLOT, SLOT), 1)

    def spread(v):
        place = v
        for k in range(1, NY):
            place = place + jnp.where(v >= OWN * k, PAD - OWN, 0)
        return jnp.where(v < DENSE, place, -1)
    sel[...] = bf16(jnp.where(col == spread(row), 1.0, 0.0))
    unsel[...] = bf16(jnp.where(row == spread(col), 1.0, 0.0))
    eye[...] = bf16(jnp.where(row == col, 1.0, 0.0))
    for s in range(NP):
        xg[s * SLOT + DENSE:(s + 1) * SLOT, :] = jnp.zeros((SLOT - DENSE, WIDE), jnp.bfloat16)
        wg[s * SLOT + DENSE:(s + 1) * SLOT, :] = jnp.zeros((SLOT - DENSE, WIDE), jnp.bfloat16)

    def in_wait(i):
        one(i, CUTS[i][1], a2a, lambda ref: copy(ref, ref, in_r.at[i], in_r.at[i], sibling).wait_recv)

    def lanes(ch):
        return slice(CUTS[ch][0], CUTS[ch][0] + CUTS[ch][1])

    class Gather:
        def __init__(self, buf, n, ch):
            self.buf, self.n, self.ch = buf, n, ch

        def ref(self, slot, part=None):
            lo, size = ((0, DENSE), (0, 176), (176, 160))[0 if part is None else part + 1]
            return self.buf.at[pl.ds(pl.multiple_of(slot * SLOT + lo, 16), size), lanes(self.ch)]

        def far(self, xx):
            return FAR + 3 * ((xx % NX) // 2)

        def push(self, q, src, dst, to):
            rsem = ag_r.at[self.n, 0 if q > 2 and self.n == 0 else self.ch, q]
            send(src, dst, ag_s.at[self.n, self.ch], rsem, to)

        def wait(self, q, ref):
            arrive(ref, ag_r.at[self.n, self.ch, q])

        def start(self):
            mine = self.ref(c)
            self.push(0, mine, self.ref(DOWN), east)
            self.push(1, mine, self.ref(UP), west)
            self.push(3, mine, mine, sibling)

        def near(self):
            self.wait(0, self.ref(DOWN))
            self.push(2, self.ref(DOWN, 0), self.ref(self.far(x + 1), 0), east)
            self.push(4, self.ref(DOWN), self.ref(DOWN_PAIR), sibling)
            self.wait(1, self.ref(UP))
            self.push(2, self.ref(UP, 1), self.ref(self.far(x + 3), 1), west)
            self.push(4, self.ref(UP), self.ref(UP_PAIR), sibling)

        def beyond(self):
            self.wait(2, self.ref(self.far(x)))
            self.push(5, self.ref(self.far(x)), self.ref(2 * FAR + 3 - self.far(x)), sibling)
            leave(self.buf.at[0:7 * DENSE, lanes(self.ch)], ag_s.at[self.n, self.ch])

        def pairs(self):
            for q, rows in ((3, 1), (4, 2), (5, 1)):
                self.wait(q, self.buf.at[0:rows * DENSE, lanes(self.ch)])

    gx = [Gather(xg, 0, ch) for ch in range(4)]
    gw = [Gather(wg, 1, ch) for ch in range(4)]

    def pairs(q):
        arrive(xg.at[0:(2 if q == 4 else 1) * DENSE, :], ag_r.at[0, 0, q])

    def mine(buf, ch):
        return buf.at[pl.ds(pl.multiple_of(c * SLOT, 16), SLOT), lanes(ch)]

    def share(ch):
        in_wait(ch)
        mine(xg, ch)[...] = bf16(dot(sel[...], a2a[:, lanes(ch)]))
        gx[ch].start()

    def gram(b):
        at = slice(b * SLOT, (b + 1) * SLOT)
        gp[:, at] = bf16(dot(a2a[...], xg[at, :], ((1,), (1,))))

    def at(q):
        return slice(STRIPS[q][0], STRIPS[q][0] + STRIPS[q][1])

    def rs_send(q, slot, t, k, to):
        send(gp.at[block(t), at(q)], rb.at[slot, :, at(q)], rs_s.at[q], rs_r.at[q, k], to)

    def rs_wait(q, k, n):
        arrive(rb.at[0:n, :, at(q)], rs_r.at[q, k])

    def add(t, q, *slots):
        v = f32(gp[block(t), at(q)])
        for slot in slots:
            v = v + f32(rb[slot, :, at(q)])
        return bf16(v)

    def rs_start(q):
        far = STRIPS[q][2]
        leave(gp.at[0:(NY - 1) * PAD, at(q)], rs_s.at[q])
        if STRIPS[q][4]:
            rs_send(q, 0, y + signs[far] * 4, 0, ydev[2 * signs[far] % NY])
            for d in range(2):
                rs_send(q, 1 + d, y + signs[d] * 3, 0, ways[d])
            for d in range(2):
                rs_send(q, 5 + d, y + signs[d], 1, ways[d])
        else:
            rs_send(q, 4 * far, y + 4, 0, ways[far])
            rs_send(q, 4 * (1 - far) + 1, y + signs[1 - far] * 3, 1, ways[1 - far])

    def rs_step(q, k):
        far = STRIPS[q][2]
        if STRIPS[q][4]:
            rs_wait(q, 0, 3)
            for d in (far, 1 - far):
                t = y + signs[d] * 2
                gp[block(t), at(q)] = add(t, q, 1 + d, 0) if d == far else add(t, q, 1 + d)
                rs_send(q, 3 + d, t, 1, ydev[2 * signs[d] % NY])
            return
        rs_wait(q, k - 1, 1 if k == 1 else 2)
        for d in range(2):
            if k == 1 and d != far:
                continue
            t = y + signs[d] * (4 - k)
            gp[block(t), at(q)] = add(t, q, 4 * d + k - 1)
            rs_send(q, 4 * d + k, t, k, ways[d])

    def rs_end(q):
        if STRIPS[q][4]:
            rs_wait(q, 1, 4)
            zs[:, at(q)] = add(y, q, 3, 4, 5, 6)
        else:
            rs_wait(q, 3, 2)
            zs[:, at(q)] = add(y, q, 3, 7)

    def gat(g, side):
        lo, _, _, shared = GROUPS[g]
        return pl.ds(pl.multiple_of(lo + side * SLOT, 128), SLOT) if shared else slice(lo, lo + SLOT)

    def z_send(g):
        theirs = gat(g, 1 - z)
        send(zs.at[:, theirs], zr.at[:, theirs], z_s.at[g], z_r.at[g], other_z)
        leave(zs.at[:, 0:SLOT], z_s.at[g])

    def mirror(g, j, side):
        ref = gf.at[block(y + j), gat(g, side)]
        if g > 0:
            b = (0, 2, 1)[g - 1]
            send(ref, mx.at[b, block(y + j), :], mx_s.at[b], mx_r.at[b], partners[b])

    def spread_on(g, k, *js):
        for j in js:
            if GROUPS[g][3]:
                ref = gf.at[block(y + j), gat(g, z)]
                send(ref, ref, zf_s.at[g], zf_r.at[g, k], other_z)
            mirror(g, j, z)

    def zf_wait(g, k, *js):
        arrive(gf.at[0:len(js) * PAD, 0:SLOT], zf_r.at[g, k])
        for j in js:
            mirror(g, j, 1 - z)

    def gg_send(g, j, k, to):
        ref = gf.at[block(y + j), gat(g, z)]
        send(ref, ref, gg_s.at[g], gg_r.at[g, k], to)

    def gg_wait(g, k, n):
        arrive(gf.at[0:n * PAD, 0:SLOT], gg_r.at[g, k])

    def gg_start(g):
        here = gat(g, z)
        arrive(zr.at[:, 0:SLOT], z_r.at[g])
        gf[block(y), here] = bf16(f32(zs[:, here]) + f32(zr[:, here]))
        leave(gf.at[0:(NY - 1) * PAD, 0:SLOT], gg_s.at[g])
        for d in range(2):
            if GROUPS[g][2]:
                gg_send(g, 0, 0, ydev[2 * signs[d] % NY])
            gg_send(g, 0, 0, ways[d])
        spread_on(g, 0, 0)
        if GROUPS[g][3]:
            leave(gf.at[:, 0:SLOT], zf_s.at[g])
        if g > 0:
            leave(gf.at[:, 0:SLOT], mx_s.at[(0, 2, 1)[g - 1]])

    def gg_step(g, k):
        far = GROUPS[g][1]
        if GROUPS[g][2]:
            gg_wait(g, 0, 4)
            for d in range(2):
                back = NY - signs[d] * 2 % NY
                if d == far:
                    gg_send(g, back, 1, ydev[2 * signs[d] % NY])
                gg_send(g, back, 1, ways[d])
            spread_on(g, 0, 1, NY - 1, 2, NY - 2)
            return
        gg_wait(g, k - 1, 2)
        for d in range(2):
            back = NY - signs[d] * k % NY
            if k < 3 or d == far:
                gg_send(g, back, k, ways[d])
            spread_on(g, 0, back)

    def gg_end(g):
        if GROUPS[g][2]:
            gg_wait(g, 1, 3)
            spread_on(g, 1, 3, NY - 3, 4)
        else:
            gg_wait(g, 3, 1)
            spread_on(g, 0, 4)

    def mirror_wait(b):
        arrive(mx.at[b], mx_r.at[b])

    def settle(b):
        at = slice(b * SLOT, (b + 1) * SLOT)
        if b < BLOCKS:
            gl[:, at] = bf16(dot(sel[...], gf[:, at]))
        else:
            turned = bf16(dot(eye[...], mx[b - BLOCKS], ((1,), (1,))))
            gl[:, at] = bf16(dot(turned, sel[...], ((1,), (1,))))

    A, B, C, D = range(4)
    share(0)
    share(1)
    share(2)
    gx[0].near()
    share(3)
    gx[1].near()
    pairs(3)
    gram(0)
    gram(1)
    rs_start(A)
    gx[2].near()
    gx[0].beyond()
    gx[3].near()
    gram(2)
    rs_start(B)
    rs_step(A, 1)
    gx[1].beyond()
    pairs(4)
    gram(3)
    rs_start(C)
    gx[2].beyond()
    gx[3].beyond()
    rs_end(A)
    z_send(0)
    rs_step(B, 1)
    pairs(5)
    gram(4)
    rs_start(D)
    rs_step(C, 1)
    gg_start(0)
    rs_end(B)
    z_send(1)
    rs_step(D, 1)
    rs_end(C)
    z_send(3)
    gg_step(0, 1)
    gg_start(1)
    rs_end(D)
    z_send(2)
    gg_start(3)
    gg_step(0, 2)
    gg_step(1, 1)
    gg_start(2)
    gg_step(3, 1)
    gg_step(0, 3)
    gg_end(1)
    gg_step(2, 1)
    gg_end(3)
    gg_end(0)
    settle(2)
    settle(3)
    gg_end(2)
    zf_wait(0, 0, *range(NY))
    settle(0)
    settle(1)
    settle(4)
    mirror_wait(0)
    settle(5)
    mirror_wait(1)
    settle(6)
    mirror_wait(2)
    settle(7)

    def inner(ch):
        v = cubic_term * f32(mine(xg, ch)[...]) + quintic_term * dot(gl[...], xg[:, lanes(ch)])
        mine(wg, ch)[...] = bf16(v)
        gw[ch].start()

    def out_copy(i, k, src, dst):
        off, size = CUTS[i]
        return copy(yp.at[block(dst), off:off + size], cut(y_ref, src, i),
                    out_s.at[i], out_r.at[i], ydev[k])

    def outer(ch):
        gw[ch].pairs()
        yp[:, lanes(ch)] = bf16(dot(unsel[...], bf16(dot(gl[...], wg[:, lanes(ch)]))))
        for k in ORDER:
            when_whole(ch, y, out_copy(ch, k, y, y + k).start)
        pending.append(lambda: one(ch, CUTS[ch][1], yp, lambda ref: copy(ref, ref, out_s.at[ch], out_s.at[ch], sibling).wait_send))

        def own():
            cut(y_ref, y, ch)[...] = yp[block(y), lanes(ch)]
        when_whole(ch, y, own)

    inner(0)
    inner(1)
    drain()
    gw[0].near()
    inner(2)
    gw[1].near()
    gw[0].beyond()
    inner(3)
    gw[2].near()
    outer(0)
    gw[1].beyond()
    gw[3].near()
    outer(1)
    gw[2].beyond()
    gw[3].beyond()
    outer(2)
    outer(3)
    for i in range(4):
        whole(i, CUTS[i][1], yp, lambda ref: copy(ref, ref, out_r.at[i], out_r.at[i], sibling).wait_recv)
    drain()


def on_device(iterate):
    bf = jnp.bfloat16
    dma = pltpu.SemaphoreType.DMA
    local = iterate.shape[1]
    n = len(STRIPS)
    applied = pl.pallas_call(
        kernel,
        out_shape=jax.ShapeDtypeStruct((PAD, local), bf),
        in_specs=[pl.BlockSpec(memory_space=pltpu.VMEM)],
        out_specs=pl.BlockSpec(memory_space=pltpu.VMEM),
        scratch_shapes=[
            pltpu.VMEM((PAD, local), bf),
            pltpu.VMEM((SLOT, SLOT), bf),
            pltpu.VMEM((SLOT, SLOT), bf),
            pltpu.VMEM((SLOT, SLOT), bf),
            pltpu.VMEM((SLOT, WIDE), bf),
            pltpu.VMEM((NP * SLOT, WIDE), bf),
            pltpu.VMEM((NP * SLOT, WIDE), bf),
            pltpu.VMEM((SLOT, SUM), bf),
            pltpu.VMEM((8, PAD, SUM), bf),
            pltpu.VMEM((PAD, SUM), bf),
            pltpu.VMEM((PAD, SUM), bf),
            pltpu.VMEM((SLOT, SUM), bf),
            pltpu.VMEM((3, SLOT, SLOT), bf),
            pltpu.VMEM((SLOT, NP * SLOT), bf),
            pltpu.VMEM((SLOT, WIDE), bf),
            dma((4,)), dma((4,)),
            dma((2, 4)), dma((2, 4, 6)),
            dma((n,)), dma((n, 4)),
            dma((4,)), dma((4,)),
            dma((4,)), dma((4, 4)),
            dma((2,)), dma((2, 2)),
            dma((3,)), dma((3,)),
            dma((4,)), dma((4,)),
        ],
        compiler_params=pltpu.CompilerParams(
            collective_id=0, has_side_effects=True, vmem_limit_bytes=50 * 2**20),
        name="newton_schulz",
    )(iterate)
    rounded = f32(iterate.astype(bf))
    return math.sqrt(COLS) * (linear_term * rounded + f32(applied[:OWN]))


def solution(mesh):
    spec = P(("mat", "row"), "col")
    return jax.shard_map(on_device, mesh=mesh, in_specs=(spec,), out_specs=spec, check_vma=False)
```

```python
import math

import jax
import jax.numpy as jnp
from jax import lax
from jax.experimental import pallas as pl
from jax.experimental.pallas import tpu as pltpu
from jax.sharding import PartitionSpec as P

COLS = 10752

linear_term = 3.4445
cubic_term = -4.775
quintic_term = 2.0315

NY = 8
NX = 4
NP = 8
OWN = 42
PAD = 48
DENSE = NY * OWN
SLOT = NY * PAD
WIDE = 768
CUTS = ((0, 256), (256, 256), (512, 128), (640, 128))
ORDER = (4, 3, 5, 2, 6, 1, 7)
UP, DOWN_PAIR, FAR, DOWN, UP_PAIR = 2, 3, 4, 5, 6
BLOCKS = 5
SUM = BLOCKS * SLOT
STRIPS = (
    (0, 768, 0, 0, True),
    (768, 384, 1, 2, True),
    (1152, 384, 0, 3, True),
    (1536, 384, 1, 4, True),
)
GROUPS = ((0, 0, False, True), (768, 1, True, False), (1536, 1, True, False), (1152, 0, True, False))


def dot(a, b, dims=((1,), (0,))):
    return lax.dot_general(a, b, (dims, ((), ())), preferred_element_type=jnp.float32)


def f32(v):
    return v.astype(jnp.float32)


def bf16(v):
    return v.astype(jnp.bfloat16)


def kernel(x_ref, y_ref, xs, sel, unsel, eye, a2a, xg, wg, gp, rb, zs, zr, gf, mx, gl, yp,
           in_s, in_r, ag_s, ag_r, rs_s, rs_r, z_s, z_r, gg_s, gg_r, zf_s, zf_r, mx_s, mx_r, out_s, out_r):
    m, r, z = lax.axis_index("mat"), lax.axis_index("row"), lax.axis_index("col")
    y, p = r // NP, r % NP
    x, c = p // 2, p % 2
    pending = []

    def dev(yy, xx, cc):
        return (m, (yy % NY) * NP + (xx % NX) * 2 + cc, z)

    def copy(src, dst, ssem, rsem, to):
        return pltpu.make_async_remote_copy(
            src_ref=src, dst_ref=dst, send_sem=ssem, recv_sem=rsem,
            device_id=to, device_id_type=pl.DeviceIdType.MESH)

    def send(src, dst, ssem, rsem, to):
        copy(src, dst, ssem, rsem, to).start()

    def arrive(ref, rsem):
        copy(ref, ref, rsem, rsem, sibling).wait_recv()

    def leave(ref, ssem):
        pending.append(copy(ref, ref, ssem, ssem, sibling).wait_send)

    def when_whole(i, yy, run):
        if i < 3:
            run()
        else:
            pl.when(yy % 4 == 3)(run)

    def whole(i, width, buf, act):
        if i < 3:
            act(buf.at[0:(NY - 1) * PAD, 0:width])()
        else:
            pl.when(y % 4 == 3)(act(buf.at[0:PAD, 0:width]))
            pl.when(y % 4 != 3)(act(buf.at[0:2 * PAD, 0:width]))

    def one(i, width, buf, act):
        when_whole(i, y, act(buf.at[0:(NY - 1) * PAD, 0:width]))

    def drain():
        for wait in pending:
            wait()
        pending.clear()

    sibling = dev(y, x, 1 - c)
    east, west = dev(y, x + 1, c), dev(y, x + 3, c)
    other_z = (m, r, 1 - z)
    ydev = [dev(y + k, x, c) for k in range(NY)]
    ways = (ydev[1], ydev[NY - 1])
    signs = (1, NY - 1)
    far_core = (c + x // 2) % 2
    partners = (east, dev(y, x + 3, 1 - c), dev(y, x + 2, far_core))
    mirrors = (west, dev(y, x + 1, 1 - c), dev(y, x + 2, 1 - far_core))

    a2a[:, 640:768] = jnp.zeros((SLOT, 128), jnp.bfloat16)
    barrier = pltpu.get_barrier_semaphore()
    greet = ydev[1:] + [sibling, east, west, other_z, partners[1], partners[2], mirrors[1], mirrors[2]]
    for to in greet:
        pl.semaphore_signal(barrier, inc=1, device_id=to, device_id_type=pl.DeviceIdType.MESH)

    xs[32:48, :] = jnp.zeros((16, xs.shape[1]), jnp.bfloat16)
    xs[0:OWN, :] = bf16(x_ref[...])
    pl.semaphore_wait(barrier, len(greet))

    def first(yy):
        return pl.multiple_of((21 * yy) // 4 * 128, 128)

    def cut(ref, yy, i):
        off, size = CUTS[i]
        return ref.at[:, pl.ds(pl.multiple_of(first(yy) + off, 128), size)]

    def block(yy):
        return pl.ds(pl.multiple_of((yy % NY) * PAD, 16), PAD)

    def in_copy(i, k, src, dst):
        off, size = CUTS[i]
        return copy(cut(xs, src, i), a2a.at[block(dst), off:off + size],
                    in_s.at[i], in_r.at[i], ydev[k])

    for i in range(4):
        for k in ORDER:
            when_whole(i, (y + k) % NY, in_copy(i, k, (y + k) % NY, y).start)
        pending.append(lambda i=i: whole(i, CUTS[i][1], a2a, lambda ref: copy(ref, ref, in_s.at[i], in_s.at[i], sibling).wait_send))

    for i, (off, size) in enumerate(CUTS):
        def own(i=i, off=off, size=size):
            a2a[block(y), off:off + size] = cut(xs, y, i)[...]
        when_whole(i, y, own)

    row = lax.broadcasted_iota(jnp.int32, (SLOT, SLOT), 0)
    col = lax.broadcasted_iota(jnp.int32, (SLOT, SLOT), 1)

    def spread(v):
        place = v
        for k in range(1, NY):
            place = place + jnp.where(v >= OWN * k, PAD - OWN, 0)
        return jnp.where(v < DENSE, place, -1)
    sel[...] = bf16(jnp.where(col == spread(row), 1.0, 0.0))
    unsel[...] = bf16(jnp.where(row == spread(col), 1.0, 0.0))
    eye[...] = bf16(jnp.where(row == col, 1.0, 0.0))
    for s in range(NP):
        xg[s * SLOT + DENSE:(s + 1) * SLOT, :] = jnp.zeros((SLOT - DENSE, WIDE), jnp.bfloat16)
        wg[s * SLOT + DENSE:(s + 1) * SLOT, :] = jnp.zeros((SLOT - DENSE, WIDE), jnp.bfloat16)

    def in_wait(i):
        one(i, CUTS[i][1], a2a, lambda ref: copy(ref, ref, in_r.at[i], in_r.at[i], sibling).wait_recv)

    def lanes(ch):
        return slice(CUTS[ch][0], CUTS[ch][0] + CUTS[ch][1])

    class Gather:
        def __init__(self, buf, n, ch):
            self.buf, self.n, self.ch = buf, n, ch

        def ref(self, slot, part=None):
            lo, size = ((0, DENSE), (0, 176), (176, 160))[0 if part is None else part + 1]
            return self.buf.at[pl.ds(pl.multiple_of(slot * SLOT + lo, 16), size), lanes(self.ch)]

        def far(self, xx):
            return FAR + 3 * ((xx % NX) // 2)

        def push(self, q, src, dst, to):
            rsem = ag_r.at[self.n, 0 if q > 2 and self.n == 0 else self.ch, q]
            send(src, dst, ag_s.at[self.n, self.ch], rsem, to)

        def wait(self, q, ref):
            arrive(ref, ag_r.at[self.n, self.ch, q])

        def start(self):
            mine = self.ref(c)
            self.push(0, mine, self.ref(DOWN), east)
            self.push(1, mine, self.ref(UP), west)
            self.push(3, mine, mine, sibling)

        def near(self):
            self.wait(0, self.ref(DOWN))
            self.push(2, self.ref(DOWN, 0), self.ref(self.far(x + 1), 0), east)
            self.push(4, self.ref(DOWN), self.ref(DOWN_PAIR), sibling)
            self.wait(1, self.ref(UP))
            self.push(2, self.ref(UP, 1), self.ref(self.far(x + 3), 1), west)
            self.push(4, self.ref(UP), self.ref(UP_PAIR), sibling)

        def beyond(self):
            self.wait(2, self.ref(self.far(x)))
            self.push(5, self.ref(self.far(x)), self.ref(2 * FAR + 3 - self.far(x)), sibling)
            leave(self.buf.at[0:7 * DENSE, lanes(self.ch)], ag_s.at[self.n, self.ch])

        def pairs(self):
            for q, rows in ((3, 1), (4, 2), (5, 1)):
                self.wait(q, self.buf.at[0:rows * DENSE, lanes(self.ch)])

    gx = [Gather(xg, 0, ch) for ch in range(4)]
    gw = [Gather(wg, 1, ch) for ch in range(4)]

    def pairs(q):
        arrive(xg.at[0:(2 if q == 4 else 1) * DENSE, :], ag_r.at[0, 0, q])

    def mine(buf, ch):
        return buf.at[pl.ds(pl.multiple_of(c * SLOT, 16), SLOT), lanes(ch)]

    def share(ch):
        in_wait(ch)
        mine(xg, ch)[...] = bf16(dot(sel[...], a2a[:, lanes(ch)]))
        gx[ch].start()

    def gram(b):
        at = slice(b * SLOT, (b + 1) * SLOT)
        gp[:, at] = bf16(dot(a2a[...], xg[at, :], ((1,), (1,))))

    def at(q):
        return slice(STRIPS[q][0], STRIPS[q][0] + STRIPS[q][1])

    def rs_send(q, slot, t, k, to):
        send(gp.at[block(t), at(q)], rb.at[slot, :, at(q)], rs_s.at[q], rs_r.at[q, k], to)

    def rs_wait(q, k, n):
        arrive(rb.at[0:n, :, at(q)], rs_r.at[q, k])

    def add(t, q, *slots):
        v = f32(gp[block(t), at(q)])
        for slot in slots:
            v = v + f32(rb[slot, :, at(q)])
        return bf16(v)

    def rs_start(q):
        far = STRIPS[q][2]
        leave(gp.at[0:(NY - 1) * PAD, at(q)], rs_s.at[q])
        if STRIPS[q][4]:
            rs_send(q, 0, y + signs[far] * 4, 0, ydev[2 * signs[far] % NY])
            for d in range(2):
                rs_send(q, 1 + d, y + signs[d] * 3, 0, ways[d])
            for d in range(2):
                rs_send(q, 5 + d, y + signs[d], 1, ways[d])
        else:
            rs_send(q, 4 * far, y + 4, 0, ways[far])
            rs_send(q, 4 * (1 - far) + 1, y + signs[1 - far] * 3, 1, ways[1 - far])

    def rs_step(q, k):
        far = STRIPS[q][2]
        if STRIPS[q][4]:
            rs_wait(q, 0, 3)
            for d in (far, 1 - far):
                t = y + signs[d] * 2
                gp[block(t), at(q)] = add(t, q, 1 + d, 0) if d == far else add(t, q, 1 + d)
                rs_send(q, 3 + d, t, 1, ydev[2 * signs[d] % NY])
            return
        rs_wait(q, k - 1, 1 if k == 1 else 2)
        for d in range(2):
            if k == 1 and d != far:
                continue
            t = y + signs[d] * (4 - k)
            gp[block(t), at(q)] = add(t, q, 4 * d + k - 1)
            rs_send(q, 4 * d + k, t, k, ways[d])

    def rs_end(q):
        if STRIPS[q][4]:
            rs_wait(q, 1, 4)
            zs[:, at(q)] = add(y, q, 3, 4, 5, 6)
        else:
            rs_wait(q, 3, 2)
            zs[:, at(q)] = add(y, q, 3, 7)

    def gat(g, side):
        lo, _, _, shared = GROUPS[g]
        return pl.ds(pl.multiple_of(lo + side * SLOT, 128), SLOT) if shared else slice(lo, lo + SLOT)

    def z_send(g):
        theirs = gat(g, 1 - z)
        send(zs.at[:, theirs], zr.at[:, theirs], z_s.at[g], z_r.at[g], other_z)
        leave(zs.at[:, 0:SLOT], z_s.at[g])

    def mirror(g, j, side):
        ref = gf.at[block(y + j), gat(g, side)]
        if g > 0:
            b = (0, 2, 1)[g - 1]
            send(ref, mx.at[b, block(y + j), :], mx_s.at[b], mx_r.at[b], partners[b])

    def spread_on(g, k, *js):
        for j in js:
            if GROUPS[g][3]:
                ref = gf.at[block(y + j), gat(g, z)]
                send(ref, ref, zf_s.at[g], zf_r.at[g, k], other_z)
            mirror(g, j, z)

    def zf_wait(g, k, *js):
        arrive(gf.at[0:len(js) * PAD, 0:SLOT], zf_r.at[g, k])
        for j in js:
            mirror(g, j, 1 - z)

    def gg_send(g, j, k, to):
        ref = gf.at[block(y + j), gat(g, z)]
        send(ref, ref, gg_s.at[g], gg_r.at[g, k], to)

    def gg_wait(g, k, n):
        arrive(gf.at[0:n * PAD, 0:SLOT], gg_r.at[g, k])

    def gg_start(g):
        here = gat(g, z)
        arrive(zr.at[:, 0:SLOT], z_r.at[g])
        gf[block(y), here] = bf16(f32(zs[:, here]) + f32(zr[:, here]))
        leave(gf.at[0:(NY - 1) * PAD, 0:SLOT], gg_s.at[g])
        for d in range(2):
            if GROUPS[g][2]:
                gg_send(g, 0, 0, ydev[2 * signs[d] % NY])
            gg_send(g, 0, 0, ways[d])
        spread_on(g, 0, 0)
        if GROUPS[g][3]:
            leave(gf.at[:, 0:SLOT], zf_s.at[g])
        if g > 0:
            leave(gf.at[:, 0:SLOT], mx_s.at[(0, 2, 1)[g - 1]])

    def gg_step(g, k):
        far = GROUPS[g][1]
        if GROUPS[g][2]:
            gg_wait(g, 0, 4)
            for d in range(2):
                back = NY - signs[d] * 2 % NY
                if d == far:
                    gg_send(g, back, 1, ydev[2 * signs[d] % NY])
                gg_send(g, back, 1, ways[d])
            spread_on(g, 0, 1, NY - 1, 2, NY - 2)
            return
        gg_wait(g, k - 1, 2)
        for d in range(2):
            back = NY - signs[d] * k % NY
            if k < 3 or d == far:
                gg_send(g, back, k, ways[d])
            spread_on(g, 0, back)

    def gg_end(g):
        if GROUPS[g][2]:
            gg_wait(g, 1, 3)
            spread_on(g, 1, 3, NY - 3, 4)
        else:
            gg_wait(g, 3, 1)
            spread_on(g, 0, 4)

    def mirror_wait(b):
        arrive(mx.at[b], mx_r.at[b])

    def settle(b):
        at = slice(b * SLOT, (b + 1) * SLOT)
        if b < BLOCKS:
            gl[:, at] = bf16(dot(sel[...], gf[:, at]))
        else:
            turned = bf16(dot(eye[...], mx[b - BLOCKS], ((1,), (1,))))
            gl[:, at] = bf16(dot(turned, sel[...], ((1,), (1,))))

    A, B, C, D = range(4)
    share(0)
    share(1)
    share(2)
    gx[0].near()
    share(3)
    pairs(3)
    gram(0)
    gram(1)
    rs_start(A)
    gx[1].near()
    gx[2].near()
    gx[0].beyond()
    gx[3].near()
    gram(2)
    rs_start(B)
    rs_step(A, 1)
    gx[1].beyond()
    pairs(4)
    gram(3)
    rs_start(C)
    gx[2].beyond()
    gx[3].beyond()
    rs_end(A)
    z_send(0)
    rs_step(B, 1)
    pairs(5)
    gram(4)
    rs_start(D)
    rs_step(C, 1)
    gg_start(0)
    rs_end(B)
    z_send(1)
    rs_step(D, 1)
    rs_end(C)
    z_send(3)
    gg_step(0, 1)
    gg_start(1)
    rs_end(D)
    z_send(2)
    gg_start(3)
    gg_step(0, 2)
    gg_step(1, 1)
    gg_start(2)
    gg_step(3, 1)
    gg_step(0, 3)
    gg_end(1)
    gg_step(2, 1)
    gg_end(3)
    gg_end(0)
    settle(2)
    settle(3)
    gg_end(2)
    zf_wait(0, 0, *range(NY))
    settle(0)
    settle(1)
    settle(4)
    mirror_wait(0)
    settle(5)
    mirror_wait(1)
    settle(6)
    mirror_wait(2)
    settle(7)

    def inner(ch):
        v = cubic_term * f32(mine(xg, ch)[...]) + quintic_term * dot(gl[...], xg[:, lanes(ch)])
        mine(wg, ch)[...] = bf16(v)
        gw[ch].start()

    def out_copy(i, k, src, dst):
        off, size = CUTS[i]
        return copy(yp.at[block(dst), off:off + size], cut(y_ref, src, i),
                    out_s.at[i], out_r.at[i], ydev[k])

    def outer(ch):
        gw[ch].pairs()
        yp[:, lanes(ch)] = bf16(dot(unsel[...], bf16(dot(gl[...], wg[:, lanes(ch)]))))
        for k in ORDER:
            when_whole(ch, y, out_copy(ch, k, y, y + k).start)
        pending.append(lambda: one(ch, CUTS[ch][1], yp, lambda ref: copy(ref, ref, out_s.at[ch], out_s.at[ch], sibling).wait_send))

        def own():
            cut(y_ref, y, ch)[...] = yp[block(y), lanes(ch)]
        when_whole(ch, y, own)

    inner(0)
    inner(1)
    drain()
    gw[0].near()
    inner(2)
    gw[1].near()
    gw[0].beyond()
    inner(3)
    gw[2].near()
    outer(0)
    gw[1].beyond()
    gw[3].near()
    outer(1)
    gw[2].beyond()
    gw[3].beyond()
    outer(2)
    outer(3)
    for i in range(4):
        whole(i, CUTS[i][1], yp, lambda ref: copy(ref, ref, out_r.at[i], out_r.at[i], sibling).wait_recv)
    drain()


def on_device(iterate):
    bf = jnp.bfloat16
    dma = pltpu.SemaphoreType.DMA
    local = iterate.shape[1]
    n = len(STRIPS)
    applied = pl.pallas_call(
        kernel,
        out_shape=jax.ShapeDtypeStruct((PAD, local), bf),
        in_specs=[pl.BlockSpec(memory_space=pltpu.VMEM)],
        out_specs=pl.BlockSpec(memory_space=pltpu.VMEM),
        scratch_shapes=[
            pltpu.VMEM((PAD, local), bf),
            pltpu.VMEM((SLOT, SLOT), bf),
            pltpu.VMEM((SLOT, SLOT), bf),
            pltpu.VMEM((SLOT, SLOT), bf),
            pltpu.VMEM((SLOT, WIDE), bf),
            pltpu.VMEM((NP * SLOT, WIDE), bf),
            pltpu.VMEM((NP * SLOT, WIDE), bf),
            pltpu.VMEM((SLOT, SUM), bf),
            pltpu.VMEM((8, PAD, SUM), bf),
            pltpu.VMEM((PAD, SUM), bf),
            pltpu.VMEM((PAD, SUM), bf),
            pltpu.VMEM((SLOT, SUM), bf),
            pltpu.VMEM((3, SLOT, SLOT), bf),
            pltpu.VMEM((SLOT, NP * SLOT), bf),
            pltpu.VMEM((SLOT, WIDE), bf),
            dma((4,)), dma((4,)),
            dma((2, 4)), dma((2, 4, 6)),
            dma((n,)), dma((n, 4)),
            dma((4,)), dma((4,)),
            dma((4,)), dma((4, 4)),
            dma((2,)), dma((2, 2)),
            dma((3,)), dma((3,)),
            dma((4,)), dma((4,)),
        ],
        compiler_params=pltpu.CompilerParams(
            collective_id=0, has_side_effects=True, vmem_limit_bytes=50 * 2**20),
        name="newton_schulz",
    )(iterate)
    rounded = f32(iterate.astype(bf))
    return math.sqrt(COLS) * (linear_term * rounded + f32(applied[:OWN]))


def solution(mesh):
    spec = P(("mat", "row"), "col")
    return jax.shard_map(on_device, mesh=mesh, in_specs=(spec,), out_specs=spec, check_vma=False)
```

```python
import math

import jax
import jax.numpy as jnp
from jax import lax
from jax.experimental import pallas as pl
from jax.experimental.pallas import tpu as pltpu
from jax.sharding import PartitionSpec as P

COLS = 10752

linear_term = 3.4445
cubic_term = -4.775
quintic_term = 2.0315

NY = 8
NX = 4
NP = 8
OWN = 42
PAD = 48
DENSE = NY * OWN
SLOT = NY * PAD
WIDE = 768
CUTS = ((0, 256), (256, 256), (512, 128), (640, 128))
ORDER = (4, 3, 5, 2, 6, 1, 7)
UP, DOWN_PAIR, FAR, DOWN, UP_PAIR = 2, 3, 4, 5, 6
BLOCKS = 5
SUM = BLOCKS * SLOT
STRIPS = (
    (0, 768, 0, 0, True),
    (768, 384, 1, 2, True),
    (1152, 384, 0, 3, True),
    (1536, 384, 1, 4, True),
)
GROUPS = ((0, 0, False, True), (768, 1, True, False), (1536, 1, True, False), (1152, 0, True, False))


def dot(a, b, dims=((1,), (0,))):
    return lax.dot_general(a, b, (dims, ((), ())), preferred_element_type=jnp.float32)


def f32(v):
    return v.astype(jnp.float32)


def bf16(v):
    return v.astype(jnp.bfloat16)


def kernel(x_ref, y_ref, xs, sel, unsel, eye, a2a, xg, wg, gp, rb, zs, zr, gf, mx, gl, yp,
           in_s, in_r, ag_s, ag_r, rs_s, rs_r, z_s, z_r, gg_s, gg_r, zf_s, zf_r, mx_s, mx_r, out_s, out_r):
    m, r, z = lax.axis_index("mat"), lax.axis_index("row"), lax.axis_index("col")
    y, p = r // NP, r % NP
    x, c = p // 2, p % 2
    pending = []

    def dev(yy, xx, cc):
        return (m, (yy % NY) * NP + (xx % NX) * 2 + cc, z)

    def copy(src, dst, ssem, rsem, to):
        return pltpu.make_async_remote_copy(
            src_ref=src, dst_ref=dst, send_sem=ssem, recv_sem=rsem,
            device_id=to, device_id_type=pl.DeviceIdType.MESH)

    def send(src, dst, ssem, rsem, to):
        copy(src, dst, ssem, rsem, to).start()

    def arrive(ref, rsem):
        copy(ref, ref, rsem, rsem, sibling).wait_recv()

    def leave(ref, ssem):
        pending.append(copy(ref, ref, ssem, ssem, sibling).wait_send)

    def when_whole(i, yy, run):
        if i < 3:
            run()
        else:
            pl.when(yy % 4 == 3)(run)

    def whole(i, width, buf, act):
        if i < 3:
            act(buf.at[0:(NY - 1) * PAD, 0:width])()
        else:
            pl.when(y % 4 == 3)(act(buf.at[0:PAD, 0:width]))
            pl.when(y % 4 != 3)(act(buf.at[0:2 * PAD, 0:width]))

    def one(i, width, buf, act):
        when_whole(i, y, act(buf.at[0:(NY - 1) * PAD, 0:width]))

    def drain():
        for wait in pending:
            wait()
        pending.clear()

    sibling = dev(y, x, 1 - c)
    east, west = dev(y, x + 1, c), dev(y, x + 3, c)
    other_z = (m, r, 1 - z)
    ydev = [dev(y + k, x, c) for k in range(NY)]
    ways = (ydev[1], ydev[NY - 1])
    signs = (1, NY - 1)
    far_core = (c + x // 2) % 2
    partners = (east, dev(y, x + 3, 1 - c), dev(y, x + 2, far_core))
    mirrors = (west, dev(y, x + 1, 1 - c), dev(y, x + 2, 1 - far_core))

    a2a[:, 640:768] = jnp.zeros((SLOT, 128), jnp.bfloat16)
    barrier = pltpu.get_barrier_semaphore()
    greet = ydev[1:] + [sibling, east, west, other_z, partners[1], partners[2], mirrors[1], mirrors[2]]
    for to in greet:
        pl.semaphore_signal(barrier, inc=1, device_id=to, device_id_type=pl.DeviceIdType.MESH)

    xs[32:48, :] = jnp.zeros((16, xs.shape[1]), jnp.bfloat16)
    xs[0:OWN, :] = bf16(x_ref[...])
    pl.semaphore_wait(barrier, len(greet))

    def first(yy):
        return pl.multiple_of((21 * yy) // 4 * 128, 128)

    def cut(ref, yy, i):
        off, size = CUTS[i]
        return ref.at[:, pl.ds(pl.multiple_of(first(yy) + off, 128), size)]

    def block(yy):
        return pl.ds(pl.multiple_of((yy % NY) * PAD, 16), PAD)

    def in_copy(i, k, src, dst):
        off, size = CUTS[i]
        return copy(cut(xs, src, i), a2a.at[block(dst), off:off + size],
                    in_s.at[i], in_r.at[i], ydev[k])

    for i in range(4):
        for k in ORDER:
            when_whole(i, (y + k) % NY, in_copy(i, k, (y + k) % NY, y).start)
        pending.append(lambda i=i: whole(i, CUTS[i][1], a2a, lambda ref: copy(ref, ref, in_s.at[i], in_s.at[i], sibling).wait_send))

    for i, (off, size) in enumerate(CUTS):
        def own(i=i, off=off, size=size):
            a2a[block(y), off:off + size] = cut(xs, y, i)[...]
        when_whole(i, y, own)

    row = lax.broadcasted_iota(jnp.int32, (SLOT, SLOT), 0)
    col = lax.broadcasted_iota(jnp.int32, (SLOT, SLOT), 1)

    def spread(v):
        place = v
        for k in range(1, NY):
            place = place + jnp.where(v >= OWN * k, PAD - OWN, 0)
        return jnp.where(v < DENSE, place, -1)
    sel[...] = bf16(jnp.where(col == spread(row), 1.0, 0.0))
    unsel[...] = bf16(jnp.where(row == spread(col), 1.0, 0.0))
    eye[...] = bf16(jnp.where(row == col, 1.0, 0.0))
    for s in range(NP):
        xg[s * SLOT + DENSE:(s + 1) * SLOT, :] = jnp.zeros((SLOT - DENSE, WIDE), jnp.bfloat16)
        wg[s * SLOT + DENSE:(s + 1) * SLOT, :] = jnp.zeros((SLOT - DENSE, WIDE), jnp.bfloat16)

    def in_wait(i):
        one(i, CUTS[i][1], a2a, lambda ref: copy(ref, ref, in_r.at[i], in_r.at[i], sibling).wait_recv)

    def lanes(ch):
        return slice(CUTS[ch][0], CUTS[ch][0] + CUTS[ch][1])

    class Gather:
        def __init__(self, buf, n, ch):
            self.buf, self.n, self.ch = buf, n, ch

        def ref(self, slot, part=None):
            lo, size = ((0, DENSE), (0, 176), (176, 160))[0 if part is None else part + 1]
            return self.buf.at[pl.ds(pl.multiple_of(slot * SLOT + lo, 16), size), lanes(self.ch)]

        def far(self, xx):
            return FAR + 3 * ((xx % NX) // 2)

        def push(self, q, src, dst, to):
            send(src, dst, ag_s.at[self.n, self.ch], ag_r.at[self.sem(q)], to)

        def sem(self, q):
            if self.n == 0:
                return self.ch * 3 + q if q < 3 else 9 + q
            return 15 + self.ch * 4 + min(q, 3)

        def wait(self, q, ref):
            arrive(ref, ag_r.at[self.sem(q)])

        def start(self):
            mine = self.ref(c)
            self.push(0, mine, self.ref(DOWN), east)
            self.push(1, mine, self.ref(UP), west)
            self.push(3, mine, mine, sibling)

        def near(self):
            self.wait(0, self.ref(DOWN))
            self.push(2, self.ref(DOWN, 0), self.ref(self.far(x + 1), 0), east)
            self.push(4, self.ref(DOWN), self.ref(DOWN_PAIR), sibling)
            self.wait(1, self.ref(UP))
            self.push(2, self.ref(UP, 1), self.ref(self.far(x + 3), 1), west)
            self.push(4, self.ref(UP), self.ref(UP_PAIR), sibling)

        def beyond(self):
            self.wait(2, self.ref(self.far(x)))
            self.push(5, self.ref(self.far(x)), self.ref(2 * FAR + 3 - self.far(x)), sibling)
            leave(self.buf.at[0:7 * DENSE, lanes(self.ch)], ag_s.at[self.n, self.ch])

        def pairs(self):
            self.wait(3, self.buf.at[0:4 * DENSE, lanes(self.ch)])

    gx = [Gather(xg, 0, ch) for ch in range(4)]
    gw = [Gather(wg, 1, ch) for ch in range(4)]

    def pairs(q):
        arrive(xg.at[0:(2 if q == 4 else 1) * DENSE, :], ag_r.at[9 + q])

    def mine(buf, ch):
        return buf.at[pl.ds(pl.multiple_of(c * SLOT, 16), SLOT), lanes(ch)]

    def share(ch):
        in_wait(ch)
        mine(xg, ch)[...] = bf16(dot(sel[...], a2a[:, lanes(ch)]))
        gx[ch].start()

    def gram(b):
        at = slice(b * SLOT, (b + 1) * SLOT)
        gp[:, at] = bf16(dot(a2a[...], xg[at, :], ((1,), (1,))))

    def at(q):
        return slice(STRIPS[q][0], STRIPS[q][0] + STRIPS[q][1])

    def rs_send(q, slot, t, k, to):
        send(gp.at[block(t), at(q)], rb.at[slot, :, at(q)], rs_s.at[q], rs_r.at[q, k], to)

    def rs_wait(q, k, n):
        arrive(rb.at[0:n, :, at(q)], rs_r.at[q, k])

    def add(t, q, *slots):
        v = f32(gp[block(t), at(q)])
        for slot in slots:
            v = v + f32(rb[slot, :, at(q)])
        return bf16(v)

    def rs_start(q):
        far = STRIPS[q][2]
        leave(gp.at[0:(NY - 1) * PAD, at(q)], rs_s.at[q])
        if STRIPS[q][4]:
            rs_send(q, 0, y + signs[far] * 4, 0, ydev[2 * signs[far] % NY])
            for d in range(2):
                rs_send(q, 1 + d, y + signs[d] * 3, 0, ways[d])
            for d in range(2):
                rs_send(q, 5 + d, y + signs[d], 1, ways[d])
        else:
            rs_send(q, 4 * far, y + 4, 0, ways[far])
            rs_send(q, 4 * (1 - far) + 1, y + signs[1 - far] * 3, 1, ways[1 - far])

    def rs_step(q, k):
        far = STRIPS[q][2]
        if STRIPS[q][4]:
            rs_wait(q, 0, 3)
            for d in (far, 1 - far):
                t = y + signs[d] * 2
                gp[block(t), at(q)] = add(t, q, 1 + d, 0) if d == far else add(t, q, 1 + d)
                rs_send(q, 3 + d, t, 1, ydev[2 * signs[d] % NY])
            return
        rs_wait(q, k - 1, 1 if k == 1 else 2)
        for d in range(2):
            if k == 1 and d != far:
                continue
            t = y + signs[d] * (4 - k)
            gp[block(t), at(q)] = add(t, q, 4 * d + k - 1)
            rs_send(q, 4 * d + k, t, k, ways[d])

    def rs_end(q):
        if STRIPS[q][4]:
            rs_wait(q, 1, 4)
            zs[:, at(q)] = add(y, q, 3, 4, 5, 6)
        else:
            rs_wait(q, 3, 2)
            zs[:, at(q)] = add(y, q, 3, 7)

    def gat(g, side):
        lo, _, _, shared = GROUPS[g]
        return pl.ds(pl.multiple_of(lo + side * SLOT, 128), SLOT) if shared else slice(lo, lo + SLOT)

    def z_send(g):
        theirs = gat(g, 1 - z)
        send(zs.at[:, theirs], zr.at[:, theirs], z_s.at[g], z_r.at[g], other_z)
        leave(zs.at[:, 0:SLOT], z_s.at[g])

    def mirror(g, j, side):
        ref = gf.at[block(y + j), gat(g, side)]
        if g > 0:
            b = (0, 2, 1)[g - 1]
            send(ref, mx.at[b, block(y + j), :], mx_s.at[b], mx_r.at[b], partners[b])

    def spread_on(g, k, *js):
        for j in js:
            if GROUPS[g][3]:
                ref = gf.at[block(y + j), gat(g, z)]
                send(ref, ref, zf_s.at[g], zf_r.at[g, k], other_z)
            mirror(g, j, z)

    def zf_wait(g, k, *js):
        arrive(gf.at[0:len(js) * PAD, 0:SLOT], zf_r.at[g, k])
        for j in js:
            mirror(g, j, 1 - z)

    def gg_send(g, j, k, to):
        ref = gf.at[block(y + j), gat(g, z)]
        send(ref, ref, gg_s.at[g], gg_r.at[k if g == 0 else 2 * g + 2 + k], to)

    def gg_wait(g, k, n):
        arrive(gf.at[0:n * PAD, 0:SLOT], gg_r.at[k if g == 0 else 2 * g + 2 + k])

    def gg_start(g):
        here = gat(g, z)
        arrive(zr.at[:, 0:SLOT], z_r.at[g])
        gf[block(y), here] = bf16(f32(zs[:, here]) + f32(zr[:, here]))
        leave(gf.at[0:(NY - 1) * PAD, 0:SLOT], gg_s.at[g])
        for d in range(2):
            if GROUPS[g][2]:
                gg_send(g, 0, 0, ydev[2 * signs[d] % NY])
            gg_send(g, 0, 0, ways[d])
        spread_on(g, 0, 0)
        if GROUPS[g][3]:
            leave(gf.at[:, 0:SLOT], zf_s.at[g])
        if g > 0:
            leave(gf.at[:, 0:SLOT], mx_s.at[(0, 2, 1)[g - 1]])

    def gg_step(g, k):
        far = GROUPS[g][1]
        if GROUPS[g][2]:
            gg_wait(g, 0, 4)
            for d in range(2):
                back = NY - signs[d] * 2 % NY
                if d == far:
                    gg_send(g, back, 1, ydev[2 * signs[d] % NY])
                gg_send(g, back, 1, ways[d])
            spread_on(g, 0, 1, NY - 1, 2, NY - 2)
            return
        gg_wait(g, k - 1, 2)
        for d in range(2):
            back = NY - signs[d] * k % NY
            if k < 3 or d == far:
                gg_send(g, back, k, ways[d])
            spread_on(g, 0, back)

    def gg_end(g):
        if GROUPS[g][2]:
            gg_wait(g, 1, 3)
            spread_on(g, 1, 3, NY - 3, 4)
        else:
            gg_wait(g, 3, 1)
            spread_on(g, 0, 4)

    def mirror_wait(b):
        arrive(mx.at[b], mx_r.at[b])

    def settle(b):
        at = slice(b * SLOT, (b + 1) * SLOT)
        if b < BLOCKS:
            gl[:, at] = bf16(dot(sel[...], gf[:, at]))
        else:
            turned = bf16(dot(eye[...], mx[b - BLOCKS], ((1,), (1,))))
            gl[:, at] = bf16(dot(turned, sel[...], ((1,), (1,))))

    A, B, C, D = range(4)
    share(0)
    share(1)
    share(2)
    gx[0].near()
    share(3)
    pairs(3)
    gram(0)
    gram(1)
    rs_start(A)
    gx[1].near()
    gx[2].near()
    gx[0].beyond()
    gx[3].near()
    gram(2)
    rs_start(B)
    rs_step(A, 1)
    gx[1].beyond()
    pairs(4)
    gram(3)
    rs_start(C)
    gx[2].beyond()
    gx[3].beyond()
    rs_end(A)
    z_send(0)
    rs_step(B, 1)
    pairs(5)
    gram(4)
    rs_start(D)
    rs_step(C, 1)
    gg_start(0)
    rs_end(B)
    z_send(1)
    rs_step(D, 1)
    rs_end(C)
    z_send(3)
    gg_step(0, 1)
    gg_start(1)
    rs_end(D)
    z_send(2)
    gg_start(3)
    gg_step(0, 2)
    gg_step(1, 1)
    gg_start(2)
    gg_step(3, 1)
    gg_step(0, 3)
    gg_end(1)
    gg_step(2, 1)
    gg_end(3)
    gg_end(0)
    settle(2)
    settle(3)
    gg_end(2)
    zf_wait(0, 0, *range(NY))
    settle(0)
    settle(1)
    settle(4)
    mirror_wait(0)
    settle(5)
    mirror_wait(1)
    settle(6)
    mirror_wait(2)
    settle(7)

    def inner(ch):
        v = cubic_term * f32(mine(xg, ch)[...]) + quintic_term * dot(gl[...], xg[:, lanes(ch)])
        mine(wg, ch)[...] = bf16(v)
        gw[ch].start()

    def out_copy(i, k, src, dst):
        off, size = CUTS[i]
        return copy(yp.at[block(dst), off:off + size], cut(y_ref, src, i),
                    out_s.at[i], out_r.at[i], ydev[k])

    def outer(ch):
        gw[ch].pairs()
        yp[:, lanes(ch)] = bf16(dot(unsel[...], bf16(dot(gl[...], wg[:, lanes(ch)]))))
        for k in ORDER:
            when_whole(ch, y, out_copy(ch, k, y, y + k).start)
        pending.append(lambda: one(ch, CUTS[ch][1], yp, lambda ref: copy(ref, ref, out_s.at[ch], out_s.at[ch], sibling).wait_send))

        def own():
            cut(y_ref, y, ch)[...] = yp[block(y), lanes(ch)]
        when_whole(ch, y, own)

    inner(0)
    inner(1)
    drain()
    gw[0].near()
    inner(2)
    gw[1].near()
    gw[0].beyond()
    inner(3)
    gw[2].near()
    outer(0)
    gw[1].beyond()
    gw[3].near()
    outer(1)
    gw[2].beyond()
    gw[3].beyond()
    outer(2)
    outer(3)
    for i in range(4):
        whole(i, CUTS[i][1], yp, lambda ref: copy(ref, ref, out_r.at[i], out_r.at[i], sibling).wait_recv)
    drain()


def on_device(iterate):
    bf = jnp.bfloat16
    dma = pltpu.SemaphoreType.DMA
    local = iterate.shape[1]
    n = len(STRIPS)
    applied = pl.pallas_call(
        kernel,
        out_shape=jax.ShapeDtypeStruct((PAD, local), bf),
        in_specs=[pl.BlockSpec(memory_space=pltpu.VMEM)],
        out_specs=pl.BlockSpec(memory_space=pltpu.VMEM),
        scratch_shapes=[
            pltpu.VMEM((PAD, local), bf),
            pltpu.VMEM((SLOT, SLOT), bf),
            pltpu.VMEM((SLOT, SLOT), bf),
            pltpu.VMEM((SLOT, SLOT), bf),
            pltpu.VMEM((SLOT, WIDE), bf),
            pltpu.VMEM((NP * SLOT, WIDE), bf),
            pltpu.VMEM((NP * SLOT, WIDE), bf),
            pltpu.VMEM((SLOT, SUM), bf),
            pltpu.VMEM((8, PAD, SUM), bf),
            pltpu.VMEM((PAD, SUM), bf),
            pltpu.VMEM((PAD, SUM), bf),
            pltpu.VMEM((SLOT, SUM), bf),
            pltpu.VMEM((3, SLOT, SLOT), bf),
            pltpu.VMEM((SLOT, NP * SLOT), bf),
            pltpu.VMEM((SLOT, WIDE), bf),
            dma((4,)), dma((4,)),
            dma((2, 4)), dma((31,)),
            dma((n,)), dma((n, 2)),
            dma((4,)), dma((4,)),
            dma((4,)), dma((10,)),
            dma((1,)), dma((1, 1)),
            dma((3,)), dma((3,)),
            dma((4,)), dma((4,)),
        ],
        compiler_params=pltpu.CompilerParams(
            collective_id=0, has_side_effects=True, vmem_limit_bytes=50 * 2**20),
        name="newton_schulz",
    )(iterate)
    rounded = f32(iterate.astype(bf))
    return math.sqrt(COLS) * (linear_term * rounded + f32(applied[:OWN]))


def solution(mesh):
    spec = P(("mat", "row"), "col")
    return jax.shard_map(on_device, mesh=mesh, in_specs=(spec,), out_specs=spec, check_vma=False)
```
